256 devices in a mesh: layer: 2 (over z_lo), row: 8 (over x, core), col: 16 (over y, z_hi).
Axes of the slice: x: 4, y: 4, z: 8 (z_hi: 4, z_lo: 2; z = z_hi * 2 + z_lo), core: 2. Of those that a mesh axis runs over, the one named last changes fastest.
Arguments:
- density: bfloat16 [512, 16, 2, 64, 64], P('row', 'col', 'layer'), as said below
- pattern: int32 [512, 16, 2], P('row', 'col', 'layer'), may hold values from -1 to 31, as said below
Outputs:
- squared: bfloat16 [512, 16, 2, 64, 64], P('row', 'col', 'layer')
- raised: bfloat16 [512, 16, 2, 64, 64], P('row', 'col', 'layer')
The draws below stay inside these ranges and needn't reach their ends.
Inputs may be any that keep to these rules, and one draw needn't show every extreme that they name: `pattern`: within one block row and column tile the non-negative entries are distinct; every block row holds 0 to 2 stored blocks in each column tile, and 2 in some. `density`: empty slots hold zero blocks.
All inputs are finite; a program needn't handle non-finite values.
Results may differ from the reference program's by a relative error of at most 0.001.
Values may be sent and summed in bfloat16 or wider, within the bound.
A program may use at most 192 MiB of HBM per device.

```python
import jax
import jax.numpy as jnp
from jax import lax

BLOCK = 64
NB = 512
SLOTS = 2
TILES = 16


def shared_pattern(key):
    width = NB // TILES
    first = jax.random.randint(jax.random.fold_in(key, 11), (NB, TILES), 0, width)
    offset = jax.random.randint(jax.random.fold_in(key, 12), (NB, TILES), 1, width)
    second = (first + offset) % width
    count = jnp.minimum(jax.random.randint(jax.random.fold_in(key, 13), (NB, TILES), 0, 4), 2)
    which = jax.random.randint(jax.random.fold_in(key, 14), (NB, TILES), 0, 2)
    empty = jnp.full((NB, TILES), -1, jnp.int32)
    slot_zero = jnp.where(count == 2, first, jnp.where((count == 1) & (which == 0), first, empty))
    slot_one = jnp.where(count == 2, second, jnp.where((count == 1) & (which == 1), first, empty))
    stacked = jnp.stack([slot_zero, slot_one], axis=-1)
    return stacked[:, :, :SLOTS].astype(jnp.int32)


def draw_pattern(key, part):
    return shared_pattern(key)


def draw_density(key, part):
    cols = shared_pattern(key)
    live = (cols >= 0).astype(jnp.float32)[:, :, :, None, None]
    shape = (NB, TILES, SLOTS, BLOCK, BLOCK)
    values = 0.35 * jax.random.normal(jax.random.fold_in(key, 21), shape, jnp.float32)
    return (values * live).astype(jnp.bfloat16)


def setup_inputs(seed: int = 0) -> dict:
    key_list = jax.random.split(jax.random.key(seed), 3)
    density = draw_density(jax.random.fold_in(key_list[2], 71), 0)
    pattern = draw_pattern(jax.random.fold_in(key_list[2], 71), 0)
    return {"density": density, "pattern": pattern}


def reference(density, pattern):
    width = NB // TILES
    flat_vals = density.reshape(NB, TILES * SLOTS, BLOCK, BLOCK)
    flat_cols = pattern.reshape(NB, TILES * SLOTS)
    owner = (jnp.arange(TILES * SLOTS, dtype=jnp.int32) // SLOTS) * width

    def one_row(index):
        a_vals = flat_vals[index].astype(jnp.float32)
        inner = jnp.clip(owner + flat_cols[index], 0, NB - 1).astype(jnp.int32)
        b_vals = density[inner].astype(jnp.float32)
        b_cols = pattern[inner]
        out_cols = pattern[index]
        match = (b_cols[:, :, None, :] == out_cols[None, :, :, None]).astype(jnp.float32)
        chosen = jnp.einsum("qtsb,qtbxy->qtsxy", match, b_vals)
        return jnp.einsum("qxy,qtsyz->tsxz", a_vals, chosen)

    full = lax.map(one_row, jnp.arange(NB, dtype=jnp.int32))
    squared = full.astype(jnp.bfloat16)
    raised = (2.0 * density.astype(jnp.float32) - full).astype(jnp.bfloat16)
    return squared, raised
```

```python
import jax
import jax.numpy as jnp
from jax import lax
from jax.experimental import pallas as pl
from jax.experimental.pallas import tpu as pltpu
from jax.sharding import PartitionSpec as P

MESH = pl.DeviceIdType.MESH
F32 = jnp.float32
BF16 = jnp.bfloat16

B = 64
W = 2 * B
HALF = 32
BODY = HALF * B
PAY = BODY + HALF
UNIT = PAY // 2
TILES = 16
YS, ZS, XS = 4, 4, 4


def lanes(rows):
    return lax.broadcasted_iota(jnp.int32, (rows, W), 1)


def gather_kernel(d_ref, p_ref, a_ref, b_ref, slots, merged,
                  ex_s, ex_r, z_s, z_r, y_s, y_r, f_s, f_r, x_s, x_r, t_s, t_r, l_s):
    layer, row, col = lax.axis_index("layer"), lax.axis_index("row"), lax.axis_index("col")
    x, core = row // 2, row % 2
    y, z = col // ZS, col % ZS
    twin = x * 2 + 1 - core

    def at_z(d):
        return y * ZS + (z + d) % ZS

    def at_y(d):
        return ((y + d) % YS) * ZS + z

    def at_x(d):
        return ((x + d) % XS) * 2 + core

    peers = [{"layer": 1 - layer}, {"row": twin}]
    peers += [{"col": at_z(d)} for d in (1, 2, 3)]
    peers += [{"col": at_y(d)} for d in (1, 3)]
    peers += [{"row": at_x(d)} for d in (1, 2, 3)]
    barrier = pltpu.get_barrier_semaphore()
    for peer in peers:
        pl.semaphore_signal(barrier, inc=1, device_id=peer, device_id_type=MESH)

    @pl.loop(0, HALF)
    def _(j):
        slots[layer, pl.ds(pl.multiple_of(j * B, B), B), :] = jnp.concatenate(
            [d_ref[j], d_ref[j + HALF]], axis=1
        )

    number = p_ref[...].astype(F32)
    lane = lax.broadcasted_iota(jnp.int32, (HALF, B), 1)
    sub = lax.broadcasted_iota(jnp.int32, (HALF, B), 0)
    low = jnp.sum(jnp.where(lane == sub, number, 0.0), axis=1, keepdims=True)
    high = jnp.sum(jnp.where(lane == sub + HALF, number, 0.0), axis=1, keepdims=True)
    slots[layer, pl.ds(BODY, HALF), :] = jnp.where(lanes(HALF) < B, low, high).astype(BF16)

    pl.semaphore_wait(barrier, len(peers))

    def part(u):
        return pl.ds(u * UNIT, UNIT)

    sends, pending = [], []

    def send(src, dst, ssem, rsem, peer):
        copy = pltpu.make_async_remote_copy(
            src_ref=src, dst_ref=dst, send_sem=ssem, recv_sem=rsem, device_id=peer, device_id_type=MESH
        )
        copy.start()
        sends.append(copy)
        return copy

    ex = [
        send(slots.at[layer, part(u)], slots.at[layer, part(u)], ex_s.at[u], ex_r.at[u], {"layer": 1 - layer})
        for u in (0, 1)
    ]

    def arrived(ref, ssem, rsem):
        pltpu.make_async_remote_copy(
            src_ref=ref, dst_ref=ref, send_sem=ssem, recv_sem=rsem, device_id={"layer": 1 - layer},
            device_id_type=MESH,
        ).wait_recv()

    mine = merged.at[layer]
    local = []
    for u in (0, 1):
        arrived(slots.at[1 - layer, part(u)], ex_s.at[u], ex_r.at[u])

        @pl.loop(0, UNIT // 16)
        def _(i):
            at = pl.ds(pl.multiple_of(u * UNIT + i * 16, 16), 16)
            one, two = slots[0, at, :], slots[1, at, :]
            left = lanes(16) < B
            swap_one = jnp.concatenate([one[:, B:], one[:, :B]], axis=1)
            swap_two = jnp.concatenate([two[:, B:], two[:, :B]], axis=1)
            merged[0, at, :] = jnp.where(left, one, swap_two)
            merged[1, at, :] = jnp.where(left, swap_one, two)

        for k, d in enumerate((1, 3)):
            send(mine.at[part(u)], a_ref.at[col, part(u)], y_s.at[0, k, u], y_r.at[0, k, u], {"col": at_y(d)})
        for d in (1, 3, 2):
            send(mine.at[part(u)], a_ref.at[col, part(u)], z_s.at[d - 1, u], z_r.at[d - 1, u], {"col": at_z(d)})
        for h in (0, 1):
            send(merged.at[h, part(u)], b_ref.at[2 * row + h, part(u)], t_s.at[h, u], t_r.at[h, u], {"row": twin})
        for d in (1, 3, 2):
            send(merged.at[core, part(u)], b_ref.at[2 * row + core, part(u)],
                 x_s.at[d - 1, 0, u], x_r.at[d - 1, 0, u], {"row": at_x(d)})
        for h in (0, 1):
            local.append(pltpu.make_async_copy(merged.at[h, part(u)], b_ref.at[2 * row + h, part(u)], l_s.at[h, u]))
        local.append(pltpu.make_async_copy(mine.at[part(u)], a_ref.at[col, part(u)], l_s.at[2, u]))
        for copy in local[-3:]:
            copy.start()

    def twin_in(h, u):
        ref = b_ref.at[2 * twin + h, part(u)]
        arrived(ref, t_s.at[h, u], t_r.at[h, u])

    def on_z(d, u):
        ref = a_ref.at[y * ZS + (z + ZS - d) % ZS, part(u)]
        arrived(ref, z_s.at[d - 1, u], z_r.at[d - 1, u])
        for k, e in enumerate((1, 3)):
            send(ref, ref, y_s.at[d, k, u], y_r.at[d, k, u], {"col": at_y(e)})

    def on_y(d, k, u):
        ref = a_ref.at[((y + (3, 1)[k]) % YS) * ZS + (z + ZS - d) % ZS, part(u)]
        arrived(ref, y_s.at[d, k, u], y_r.at[d, k, u])
        if k == u:
            send(ref, ref, f_s.at[d, k], f_r.at[d, k], {"col": at_y((1, 3)[k])})

    def on_f(d, k):
        ref = a_ref.at[((y + 2) % YS) * ZS + (z + ZS - d) % ZS, part(k)]
        arrived(ref, f_s.at[d, k], f_r.at[d, k])

    def on_x(d, p, u):
        there = ((x + XS - d) % XS) * 2 + (core if p == 0 else 1 - core)
        ref = b_ref.at[2 * there + core, part(u)]
        arrived(ref, x_s.at[d - 1, p, u], x_r.at[d - 1, p, u])
        n = 2 + (d - 1) * 2 + p
        send(ref, ref, t_s.at[n, u], t_r.at[n, u], {"row": twin})

    for u in (0, 1):
        twin_in(0, u)
        twin_in(1, u)
        for d in (1, 3, 2):
            ref = b_ref.at[2 * twin + core, part(u)]
            send(ref, ref, x_s.at[d - 1, 1, u], x_r.at[d - 1, 1, u], {"row": at_x(d)})
    for u in (0, 1):
        on_y(0, 0, u)
        on_y(0, 1, u)
        on_z(1, u)
        on_z(3, u)
    for u in (0, 1):
        on_x(1, 0, u)
        on_x(3, 0, u)
        on_z(2, u)
    for u in (0, 1):
        for d in (1, 3):
            on_y(d, 0, u)
            on_y(d, 1, u)
        on_x(1, 1, u)
        on_x(3, 1, u)
        on_x(2, 0, u)
        on_x(2, 1, u)
    for u in (0, 1):
        on_y(2, 0, u)
        on_y(2, 1, u)
    for d in (0, 1, 3, 2):
        on_f(d, 0)
        on_f(d, 1)
    for d in (1, 2, 3):
        for p in (0, 1):
            there = ((x + XS - d) % XS) * 2 + (1 - core if p == 0 else core)
            n = 2 + (d - 1) * 2 + p
            for u in (0, 1):
                arrived(b_ref.at[2 * there + 1 - core, part(u)], t_s.at[n, u], t_r.at[n, u])
    for copy in sends:
        copy.wait_send()
    for copy in local:
        copy.wait()


def gather(d, p):
    wide = jax.ShapeDtypeStruct((TILES, PAY, W), BF16)
    dma = pltpu.SemaphoreType.DMA
    return pl.pallas_call(
        gather_kernel,
        out_shape=(wide, wide),
        in_specs=[pl.BlockSpec(memory_space=pltpu.VMEM)] * 2,
        out_specs=(pl.BlockSpec(memory_space=pl.ANY),) * 2,
        scratch_shapes=[
            pltpu.VMEM((2, PAY, W), BF16),
            pltpu.VMEM((2, PAY, W), BF16),
            dma((2,)), dma((2,)),
            dma((3, 2)), dma((3, 2)),
            dma((4, 2, 2)), dma((4, 2, 2)),
            dma((4, 2)), dma((4, 2)),
            dma((3, 2, 2)), dma((3, 2, 2)),
            dma((8, 2)), dma((8, 2)),
            dma((3, 2)),
        ],
        compiler_params=pltpu.CompilerParams(
            collective_id=0, has_side_effects=True, vmem_limit_bytes=12 << 20
        ),
        name="gather",
    )(d, p)


def multiply_kernel(a_ref, b_ref, o_ref, acc, codes, scalars, sem):
    col = lax.axis_index("col")
    sub = lax.broadcasted_iota(jnp.int32, (HALF, W), 0)
    place = lanes(HALF) % B

    def in_row(block):
        return jnp.sum(jnp.where(place == sub, block, 0.0), axis=0, keepdims=True)

    def turn(v):
        return jnp.concatenate([v[:, B:], v[:, :B]], axis=1)

    want = in_row(a_ref[col, pl.ds(BODY, HALF), :].astype(F32))
    want_turned = turn(want)
    right = lanes(1) >= B
    used = lanes(1) % B < HALF
    for t in range(TILES):
        inner = in_row(a_ref[t, pl.ds(BODY, HALF), :].astype(F32))
        table = b_ref[t, pl.ds(BODY, HALF), :].astype(F32)
        hot = inner == sub.astype(F32)
        own = jnp.sum(jnp.where(hot, table, 0.0), axis=0, keepdims=True)
        other = jnp.sum(jnp.where(hot, turn(table), 0.0), axis=0, keepdims=True)
        live = used & (inner >= 0)

        def same(u, v):
            return jnp.where(live & (u == v) & (v >= 0), 1, 0)

        f0, f1 = same(own, want), same(other, want)
        f2, f3 = same(own, want_turned), same(other, want_turned)
        flags = (
            jnp.where(right, f3, f0) + 2 * jnp.where(right, f0, f3)
            + 4 * jnp.where(right, f2, f1) + 8 * jnp.where(right, f1, f2)
        )
        codes[pl.ds(t, 1), :] = jnp.where(flags > 0, flags + 16 * inner.astype(jnp.int32), 0)
    copy = pltpu.make_async_copy(codes, scalars, sem)
    copy.start()

    @pl.loop(0, HALF)
    def _(j):
        acc[j] = jnp.zeros((B, W), F32)

    copy.wait()

    @pl.loop(0, TILES)
    def _(t):
        for s in (0, 1):
            @pl.loop(0, HALF, unroll=8)
            def _(j):
                code = scalars[t, s * B + j]

                @pl.when(code > 0)
                def _():
                    k = code // 16
                    left = lanes(1) < B

                    def pick(bit_left, bit_right):
                        return jnp.where(left, (code // bit_left) % 2, (code // bit_right) % 2).astype(F32)

                    v = b_ref[t, pl.ds(pl.multiple_of(k * B, B), B), :].astype(F32)
                    w = (v * pick(1, 2) + turn(v) * pick(4, 8)).astype(BF16)
                    a = a_ref[t, pl.ds(pl.multiple_of(j * B, B), B), :]
                    acc[j] += jnp.dot(a[:, s * B:(s + 1) * B], w, preferred_element_type=F32)

    @pl.loop(0, HALF)
    def _(j):
        full = acc[j]
        mine = a_ref[col, pl.ds(pl.multiple_of(j * B, B), B), :].astype(F32)
        squared = full
        raised = 2.0 * mine - full
        left = lanes(B) < B
        o_ref[0, j] = jnp.where(left, squared, turn(raised)).astype(BF16)
        o_ref[1, j] = jnp.where(left, turn(squared), raised).astype(BF16)


def multiply(a, b):
    return pl.pallas_call(
        multiply_kernel,
        out_shape=jax.ShapeDtypeStruct((2, HALF, B, W), BF16),
        in_specs=[pl.BlockSpec(memory_space=pltpu.VMEM)] * 2,
        out_specs=pl.BlockSpec(memory_space=pltpu.VMEM),
        scratch_shapes=[
            pltpu.VMEM((HALF, B, W), F32),
            pltpu.VMEM((TILES, W), jnp.int32),
            pltpu.SMEM((TILES, W), jnp.int32),
            pltpu.SemaphoreType.DMA,
        ],
        compiler_params=pltpu.CompilerParams(vmem_limit_bytes=32 << 20),
        name="multiply",
    )(a, b)


CUTS = 4


def swap_kernel(o_ref, sq_ref, ra_ref, got, s_sem, r_sem):
    layer = lax.axis_index("layer")
    other = {"layer": 1 - layer}
    barrier = pltpu.get_barrier_semaphore()
    pl.semaphore_signal(barrier, inc=1, device_id=other, device_id_type=MESH)
    pl.semaphore_wait(barrier, 1)
    size = HALF // CUTS
    copies = []
    for n in range(CUTS):
        at = pl.ds(n * size, size)
        copy = pltpu.make_async_remote_copy(
            src_ref=o_ref.at[1 - layer, at], dst_ref=got.at[at], send_sem=s_sem.at[n], recv_sem=r_sem.at[n],
            device_id=other, device_id_type=MESH,
        )
        copy.start()
        copies.append(copy)

    @pl.loop(0, HALF)
    def _(j):
        both = o_ref[layer, j]
        sq_ref[layer * HALF + j] = both[:, :B]
        ra_ref[layer * HALF + j] = both[:, B:]

    for n, copy in enumerate(copies):
        copy.wait_recv()

        @pl.loop(n * size, (n + 1) * size)
        def _(j):
            both = got[j]
            sq_ref[(1 - layer) * HALF + j] = both[:, :B]
            ra_ref[(1 - layer) * HALF + j] = both[:, B:]

    for copy in copies:
        copy.wait_send()


def swap(o):
    out = jax.ShapeDtypeStruct((2 * HALF, B, B), BF16)
    return pl.pallas_call(
        swap_kernel,
        out_shape=(out, out),
        in_specs=[pl.BlockSpec(memory_space=pltpu.VMEM)],
        out_specs=(pl.BlockSpec(memory_space=pltpu.VMEM),) * 2,
        scratch_shapes=[
            pltpu.VMEM((HALF, B, W), BF16),
            pltpu.SemaphoreType.DMA((CUTS,)),
            pltpu.SemaphoreType.DMA((CUTS,)),
        ],
        compiler_params=pltpu.CompilerParams(
            collective_id=1, has_side_effects=True, vmem_limit_bytes=12 << 20
        ),
        name="swap",
    )(o)


def on_device(density, pattern):
    a, b = gather(density.reshape(2 * HALF, B, B), pattern.reshape(1, 2 * HALF))
    squared, raised = swap(multiply(a, b))
    return squared.reshape(density.shape), raised.reshape(density.shape)


def solution(mesh):
    placed = (P("row", "col", "layer", None, None), P("row", "col", "layer"))
    return jax.shard_map(
        on_device,
        mesh=mesh,
        in_specs=placed,
        out_specs=(P("row", "col", "layer", None, None), P("row", "col", "layer", None, None)),
        check_vma=False,
    )
```

```python
import jax
import jax.numpy as jnp
from jax import lax
from jax.experimental import pallas as pl
from jax.experimental.pallas import tpu as pltpu
from jax.sharding import PartitionSpec as P

MESH = pl.DeviceIdType.MESH
F32 = jnp.float32
BF16 = jnp.bfloat16

B = 64
W = 2 * B
HALF = 32
PAIRS = HALF // 2
BODY = PAIRS * B
UNIT = BODY + PAIRS
TILES = 16
YS, ZS, XS = 4, 4, 4


def lanes(rows):
    return lax.broadcasted_iota(jnp.int32, (rows, W), 1)


def gather_kernel(d_ref, p_ref, a_ref, b_ref,
                  e_s, e_r, z_s, z_r, y_s, y_r, f_s, f_r, g_s, g_r, x_s, x_r, t_s, t_r, l_s):
    layer, row, col = lax.axis_index("layer"), lax.axis_index("row"), lax.axis_index("col")
    x, core = row // 2, row % 2
    y, z = col // ZS, col % ZS
    twin = x * 2 + 1 - core
    step, away = 1 + 2 * core, 3 - 2 * layer

    def at_z(d):
        return y * ZS + (z + d) % ZS

    def at_y(d):
        return ((y + d) % YS) * ZS + z

    def at_x(d):
        return ((x + d) % XS) * 2 + core

    other = {"layer": 1 - layer}
    aside = {"layer": 1 - layer, "col": at_z(away)}
    peers = [other, aside, {"row": twin}]
    peers += [{"col": at_z(d)} for d in (1, 3)]
    peers += [{"col": at_y(d)} for d in (1, 3)]
    peers += [{"row": at_x(d)} for d in (1, 2, 3)]
    barrier = pltpu.get_barrier_semaphore()
    for peer in peers:
        pl.semaphore_signal(barrier, inc=1, device_id=peer, device_id_type=MESH)

    number = p_ref[...].astype(F32)
    lane = lax.broadcasted_iota(jnp.int32, (PAIRS, B), 1)
    sub = lax.broadcasted_iota(jnp.int32, (PAIRS, B), 0)

    def entry(first):
        return jnp.sum(jnp.where(lane == sub + first, number, 0.0), axis=1, keepdims=True)

    for h in (0, 1):
        @pl.loop(0, PAIRS)
        def _(j):
            b_ref[2 * row + h, layer, pl.ds(pl.multiple_of(j * B, B), B), :] = jnp.concatenate(
                [d_ref[h * HALF + j], d_ref[h * HALF + PAIRS + j]], axis=1
            )

        b_ref[2 * row + h, layer, pl.ds(BODY, PAIRS), :] = jnp.where(
            lanes(PAIRS) < B, entry(h * HALF), entry(h * HALF + PAIRS)
        ).astype(BF16)

    pl.semaphore_wait(barrier, len(peers))

    sends, local = [], []

    def send(src, dst, ssem, rsem, peer):
        copy = pltpu.make_async_remote_copy(
            src_ref=src, dst_ref=dst, send_sem=ssem, recv_sem=rsem, device_id=peer, device_id_type=MESH
        )
        copy.start()
        sends.append(copy)

    def arrived(ref, ssem, rsem):
        pltpu.make_async_remote_copy(
            src_ref=ref, dst_ref=ref, send_sem=ssem, recv_sem=rsem, device_id=other, device_id_type=MESH
        ).wait_recv()

    offset = (0, 4 - step, step, 0, away, 4 - away, 2, 2)
    whose = (layer, layer, layer, 1 - layer, 1 - layer, 1 - layer, 1 - layer, layer)

    def a_at(dy, n):
        return a_ref.at[((y + dy) % YS) * ZS + (z + offset[n]) % ZS, whose[n]]

    def b_at(there, h, s):
        return b_ref.at[2 * there + h, s]

    mine, theirs = b_at(row, layer, layer), b_at(row, 1 - layer, layer)

    def sense(n):
        return 1 + 2 * ((n + core) % 2)

    def to_y(src, n):
        for k, d in enumerate((sense(n), 4 - sense(n))):
            send(src, a_at(0, n), y_s.at[n, k], y_r.at[n, k], {"col": at_y(d)})

    def to_x(src, h, own):
        n = h * 2 + own
        for d in (1, 3, 2):
            send(src, src, x_s.at[n, d - 1], x_r.at[n, d - 1], {"row": at_x(d)})

    def to_twin(src, n):
        send(src, src, t_s.at[n], t_r.at[n], {"row": twin})

    def keep(src, n):
        copy = pltpu.make_async_copy(src, a_at(0, n), l_s.at[n // 3])
        copy.start()
        local.append(copy)

    def pass_far(ref, m):
        send(ref, ref, g_s.at[m], g_r.at[m], {"col": at_z(step)})

    to_y(mine, 0)
    send(theirs, theirs, z_s.at[3], z_r.at[3], other)
    send(mine, a_at(0, 0), z_s.at[1], z_r.at[1], {"col": at_z(step)})
    send(theirs, a_at(0, 0), z_s.at[4], z_r.at[4], aside)
    send(mine, a_at(0, 0), z_s.at[2], z_r.at[2], {"col": at_z(4 - step)})
    to_x(mine, 0, 0)
    to_x(theirs, 1, 0)
    to_twin(mine, 0)
    to_twin(theirs, 2)
    keep(mine, 0)

    def on_z(n):
        if n == 3:
            ref = b_at(row, layer, 1 - layer)
            arrived(ref, z_s.at[n], z_r.at[n])
            send(ref, a_at(0, 3), z_s.at[5], z_r.at[5], {"col": at_z(away)})
        else:
            ref = a_at(0, n)
            arrived(ref, z_s.at[n], z_r.at[n])
            if n == 1:
                pass_far(ref, 0)
            if n == 4:
                send(ref, ref, z_s.at[6], z_r.at[6], {"col": at_z(4 - away)})
        to_y(ref, n)
        if n == 3:
            to_x(ref, 0, 1)
            to_twin(ref, 1)
            keep(ref, 3)

    def on_y(n, k):
        d = (4 - sense(n), sense(n))[k]
        ref = a_at(d, n)
        arrived(ref, y_s.at[n, k], y_r.at[n, k])
        if n == 1:
            pass_far(ref, 1 + k)
        if k == 0:
            send(ref, ref, f_s.at[n], f_r.at[n], {"col": at_y(sense(n))})

    def on_f(n):
        ref = a_at(2, n)
        arrived(ref, f_s.at[n], f_r.at[n])
        if n == 1:
            pass_far(ref, 3)

    def on_far(m):
        arrived(a_at((0, 4 - sense(1), sense(1), 2)[m], 7), g_s.at[m], g_r.at[m])

    def on_x(d, h, own):
        there = ((x + XS - d) % XS) * 2 + core
        ref = b_at(there, (layer, 1 - layer)[h], (layer, 1 - layer)[own])
        n = h * 2 + own
        arrived(ref, x_s.at[n, d - 1], x_r.at[n, d - 1])
        to_twin(ref, 4 + n * 3 + d - 1)

    on_z(3)
    on_z(1)
    on_y(0, 0)
    on_z(4)
    send(mine, mine, e_s, e_r, other)
    on_y(0, 1)
    on_y(3, 0)
    on_y(1, 0)
    on_y(1, 1)
    on_z(2)
    for d in (1, 3):
        on_x(d, 0, 0)
    on_y(4, 0)
    on_f(1)
    on_z(5)
    on_z(6)
    for d in (1, 3):
        on_x(d, 1, 0)
    ref = b_at(row, 1 - layer, 1 - layer)
    arrived(ref, e_s, e_r)
    to_x(ref, 1, 1)
    to_twin(ref, 3)
    on_y(2, 0)
    on_x(2, 0, 0)
    on_x(2, 1, 0)
    on_y(5, 0)
    for d in (1, 3, 2):
        on_x(d, 0, 1)
    on_y(6, 0)
    for d in (1, 3, 2):
        on_x(d, 1, 1)
    for n in (3, 4, 2, 5, 6):
        on_y(n, 1)
    for n in (0, 3, 4, 2, 5, 6):
        on_f(n)
    for m in range(4):
        on_far(m)
    for n in range(4):
        h, s = (layer, 1 - layer)[n // 2], (layer, 1 - layer)[n % 2]
        arrived(b_at(twin, h, s), t_s.at[n], t_r.at[n])
        for d in (1, 2, 3):
            there = ((x + XS - d) % XS) * 2 + 1 - core
            m = 4 + n * 3 + d - 1
            arrived(b_at(there, h, s), t_s.at[m], t_r.at[m])
    for copy in sends:
        copy.wait_send()
    for copy in local:
        copy.wait()


def gather(d, p):
    wide = jax.ShapeDtypeStruct((TILES, 2, UNIT, W), BF16)
    dma = pltpu.SemaphoreType.DMA
    return pl.pallas_call(
        gather_kernel,
        out_shape=(wide, wide),
        in_specs=[pl.BlockSpec(memory_space=pltpu.VMEM)] * 2,
        out_specs=(pl.BlockSpec(memory_space=pltpu.VMEM),) * 2,
        scratch_shapes=[
            dma, dma,
            dma((7,)), dma((7,)),
            dma((7, 2)), dma((7, 2)),
            dma((7,)), dma((7,)),
            dma((4,)), dma((4,)),
            dma((4, 3)), dma((4, 3)),
            dma((16,)), dma((16,)),
            dma((2,)),
        ],
        compiler_params=pltpu.CompilerParams(
            collective_id=0, has_side_effects=True, vmem_limit_bytes=30 << 20
        ),
        name="gather",
    )(d, p)


def multiply_kernel(a_ref, b_ref, o_ref, acc, codes, scalars, sem):
    col = lax.axis_index("col")
    sub = lax.broadcasted_iota(jnp.int32, (HALF, W), 0)
    place = lanes(HALF) % B

    def turn(v):
        return jnp.concatenate([v[:, B:], v[:, :B]], axis=1)

    def pattern(ref, t):
        one = ref[t, 0, pl.ds(BODY, PAIRS), :].astype(F32)
        two = ref[t, 1, pl.ds(BODY, PAIRS), :].astype(F32)
        left = lanes(PAIRS) < B
        return jnp.concatenate([jnp.where(left, one, turn(two)), jnp.where(left, turn(one), two)], axis=0)

    def in_row(block):
        return jnp.sum(jnp.where(place == sub, block, 0.0), axis=0, keepdims=True)

    want = in_row(pattern(a_ref, col))
    want_turned = turn(want)
    right = lanes(1) >= B
    used = lanes(1) % B < HALF
    for t in range(TILES):
        inner = in_row(pattern(a_ref, t))
        table = pattern(b_ref, t)
        hot = inner == sub.astype(F32)
        own = jnp.sum(jnp.where(hot, table, 0.0), axis=0, keepdims=True)
        other = jnp.sum(jnp.where(hot, turn(table), 0.0), axis=0, keepdims=True)
        live = used & (inner >= 0)

        def same(u, v):
            return jnp.where(live & (u == v) & (v >= 0), 1, 0)

        f0, f1 = same(own, want), same(other, want)
        f2, f3 = same(own, want_turned), same(other, want_turned)
        flags = (
            jnp.where(right, f3, f0) + 2 * jnp.where(right, f0, f3)
            + 4 * jnp.where(right, f2, f1) + 8 * jnp.where(right, f1, f2)
        )
        codes[pl.ds(t, 1), :] = jnp.where(flags > 0, flags + 16 * inner.astype(jnp.int32), 0)
    copy = pltpu.make_async_copy(codes, scalars, sem)
    copy.start()

    @pl.loop(0, HALF)
    def _(j):
        acc[j] = jnp.zeros((B, W), F32)

    copy.wait()
    left = lanes(1) < B

    @pl.loop(0, TILES)
    def _(t):
        for s in (0, 1):
            for q in (0, 1):
                @pl.loop(0, PAIRS, unroll=8)
                def _(j):
                    code = scalars[t, s * B + q * PAIRS + j]

                    @pl.when(code > 0)
                    def _():
                        k = code // 16
                        at = pl.ds(pl.multiple_of(k % PAIRS * B, B), B)
                        far = k // PAIRS

                        def pick(bit_left, bit_right):
                            return jnp.where(left, (code // bit_left) % 2, (code // bit_right) % 2).astype(F32)

                        def shifted(v, by):
                            return jnp.where(by == 1, turn(v), v)

                        one, two = b_ref[t, 0, at, :].astype(F32), b_ref[t, 1, at, :].astype(F32)
                        v = jnp.where(left, shifted(one, far), shifted(two, 1 - far))
                        w = (v * pick(1, 2) + turn(v) * pick(4, 8)).astype(BF16)
                        a = a_ref[t, s, pl.ds(pl.multiple_of(j * B, B), B), :]
                        acc[q * PAIRS + j] += jnp.dot(a[:, q * B:(q + 1) * B], w, preferred_element_type=F32)

    @pl.loop(0, PAIRS)
    def _(j):
        at = pl.ds(pl.multiple_of(j * B, B), B)
        one, two = a_ref[col, 0, at, :].astype(F32), a_ref[col, 1, at, :].astype(F32)
        for q in (0, 1):
            full = acc[q * PAIRS + j]
            mine = jnp.where(left, one, turn(two)) if q == 0 else jnp.where(left, turn(one), two)
            raised = 2.0 * mine - full
            o_ref[0, q * PAIRS + j] = jnp.where(left, full, turn(raised)).astype(BF16)
            o_ref[1, q * PAIRS + j] = jnp.where(left, turn(full), raised).astype(BF16)


def multiply(a, b):
    return pl.pallas_call(
        multiply_kernel,
        out_shape=jax.ShapeDtypeStruct((2, HALF, B, W), BF16),
        in_specs=[pl.BlockSpec(memory_space=pltpu.VMEM)] * 2,
        out_specs=pl.BlockSpec(memory_space=pltpu.VMEM),
        scratch_shapes=[
            pltpu.VMEM((HALF, B, W), F32),
            pltpu.VMEM((TILES, W), jnp.int32),
            pltpu.SMEM((TILES, W), jnp.int32),
            pltpu.SemaphoreType.DMA,
        ],
        compiler_params=pltpu.CompilerParams(vmem_limit_bytes=32 << 20),
        name="multiply",
    )(a, b)


CUTS = 4


def swap_kernel(o_ref, sq_ref, ra_ref, got, s_sem, r_sem):
    layer = lax.axis_index("layer")
    other = {"layer": 1 - layer}
    barrier = pltpu.get_barrier_semaphore()
    pl.semaphore_signal(barrier, inc=1, device_id=other, device_id_type=MESH)
    pl.semaphore_wait(barrier, 1)
    size = HALF // CUTS
    copies = []
    for n in range(CUTS):
        at = pl.ds(n * size, size)
        copy = pltpu.make_async_remote_copy(
            src_ref=o_ref.at[1 - layer, at], dst_ref=got.at[at], send_sem=s_sem.at[n], recv_sem=r_sem.at[n],
            device_id=other, device_id_type=MESH,
        )
        copy.start()
        copies.append(copy)

    @pl.loop(0, HALF)
    def _(j):
        both = o_ref[layer, j]
        sq_ref[layer * HALF + j] = both[:, :B]
        ra_ref[layer * HALF + j] = both[:, B:]

    for n, copy in enumerate(copies):
        copy.wait_recv()

        @pl.loop(n * size, (n + 1) * size)
        def _(j):
            both = got[j]
            sq_ref[(1 - layer) * HALF + j] = both[:, :B]
            ra_ref[(1 - layer) * HALF + j] = both[:, B:]

    for copy in copies:
        copy.wait_send()


def swap(o):
    out = jax.ShapeDtypeStruct((2 * HALF, B, B), BF16)
    return pl.pallas_call(
        swap_kernel,
        out_shape=(out, out),
        in_specs=[pl.BlockSpec(memory_space=pltpu.VMEM)],
        out_specs=(pl.BlockSpec(memory_space=pltpu.VMEM),) * 2,
        scratch_shapes=[
            pltpu.VMEM((HALF, B, W), BF16),
            pltpu.SemaphoreType.DMA((CUTS,)),
            pltpu.SemaphoreType.DMA((CUTS,)),
        ],
        compiler_params=pltpu.CompilerParams(
            collective_id=1, has_side_effects=True, vmem_limit_bytes=12 << 20
        ),
        name="swap",
    )(o)


def on_device(density, pattern):
    a, b = gather(density.reshape(2 * HALF, B, B), pattern.reshape(1, 2 * HALF))
    squared, raised = swap(multiply(a, b))
    return squared.reshape(density.shape), raised.reshape(density.shape)


def solution(mesh):
    placed = (P("row", "col", "layer", None, None), P("row", "col", "layer"))
    return jax.shard_map(
        on_device,
        mesh=mesh,
        in_specs=placed,
        out_specs=(P("row", "col", "layer", None, None), P("row", "col", "layer", None, None)),
        check_vma=False,
    )
```

```python
import jax
import jax.numpy as jnp
from jax import lax
from jax.experimental import pallas as pl
from jax.experimental.pallas import tpu as pltpu
from jax.sharding import PartitionSpec as P

MESH = pl.DeviceIdType.MESH
F32 = jnp.float32
BF16 = jnp.bfloat16

B = 64
W = 2 * B
HALF = 32
PAIRS = HALF // 2
BODY = PAIRS * B
UNIT = BODY + PAIRS
TILES = 16
YS, ZS, XS = 4, 4, 4


def lanes(rows):
    return lax.broadcasted_iota(jnp.int32, (rows, W), 1)


def gather_kernel(d_ref, p_ref, a_ref, b_ref,
                  e_s, e_r, z_s, z_r, y_s, y_r, f_s, f_r, g_s, g_r, x_s, x_r, t_s, t_r, l_s):
    layer, row, col = lax.axis_index("layer"), lax.axis_index("row"), lax.axis_index("col")
    x, core = row // 2, row % 2
    y, z = col // ZS, col % ZS
    twin = x * 2 + 1 - core
    step, away = 1 + 2 * core, 3 - 2 * layer

    def at_z(d):
        return y * ZS + (z + d) % ZS

    def at_y(d):
        return ((y + d) % YS) * ZS + z

    def at_x(d):
        return ((x + d) % XS) * 2 + core

    other = {"layer": 1 - layer}
    aside = {"layer": 1 - layer, "col": at_z(away)}
    peers = [other, aside, {"row": twin}]
    peers += [{"col": at_z(d)} for d in (1, 3)]
    peers += [{"col": at_y(d)} for d in (1, 3)]
    peers += [{"row": at_x(d)} for d in (1, 2, 3)]
    barrier = pltpu.get_barrier_semaphore()
    for peer in peers:
        pl.semaphore_signal(barrier, inc=1, device_id=peer, device_id_type=MESH)

    number = p_ref[...].astype(F32)
    lane = lax.broadcasted_iota(jnp.int32, (PAIRS, B), 1)
    sub = lax.broadcasted_iota(jnp.int32, (PAIRS, B), 0)

    def entry(first):
        return jnp.sum(jnp.where(lane == sub + first, number, 0.0), axis=1, keepdims=True)

    for h in (0, 1):
        @pl.loop(0, PAIRS)
        def _(j):
            b_ref[2 * row + h, layer, pl.ds(pl.multiple_of(j * B, B), B), :] = jnp.concatenate(
                [d_ref[h * HALF + j], d_ref[h * HALF + PAIRS + j]], axis=1
            )

        b_ref[2 * row + h, layer, pl.ds(BODY, PAIRS), :] = jnp.where(
            lanes(PAIRS) < B, entry(h * HALF), entry(h * HALF + PAIRS)
        ).astype(BF16)

    pl.semaphore_wait(barrier, len(peers))

    sends, local = [], []

    def send(src, dst, ssem, rsem, peer):
        copy = pltpu.make_async_remote_copy(
            src_ref=src, dst_ref=dst, send_sem=ssem, recv_sem=rsem, device_id=peer, device_id_type=MESH
        )
        copy.start()
        sends.append(copy)

    def arrived(ref, ssem, rsem):
        pltpu.make_async_remote_copy(
            src_ref=ref, dst_ref=ref, send_sem=ssem, recv_sem=rsem, device_id=other, device_id_type=MESH
        ).wait_recv()

    offset = (0, 4 - step, step, 0, away, 4 - away, 2, 2)
    whose = (layer, layer, layer, 1 - layer, 1 - layer, 1 - layer, 1 - layer, layer)

    def a_at(dy, n):
        return a_ref.at[((y + dy) % YS) * ZS + (z + offset[n]) % ZS, whose[n]]

    def b_at(there, h, s):
        return b_ref.at[2 * there + h, s]

    mine, theirs = b_at(row, layer, layer), b_at(row, 1 - layer, layer)

    def sense(n):
        return 1 + 2 * ((n + core) % 2)

    def to_y(src, n):
        for k, d in enumerate((sense(n), 4 - sense(n))):
            send(src, a_at(0, n), y_s.at[n, k], y_r.at[n, k], {"col": at_y(d)})

    def to_x(src, h, own):
        n = h * 2 + own
        for d in (1, 3, 2):
            send(src, src, x_s.at[n, d - 1], x_r.at[n, d - 1], {"row": at_x(d)})

    def to_twin(src, n):
        send(src, src, t_s.at[n], t_r.at[n], {"row": twin})

    def keep(src, n):
        copy = pltpu.make_async_copy(src, a_at(0, n), l_s.at[n // 3])
        copy.start()
        local.append(copy)

    def pass_far(ref, m):
        send(ref, ref, g_s.at[m], g_r.at[m], {"col": at_z(step)})

    to_y(mine, 0)
    send(theirs, theirs, z_s.at[3], z_r.at[3], other)
    send(mine, a_at(0, 0), z_s.at[1], z_r.at[1], {"col": at_z(step)})
    send(theirs, a_at(0, 0), z_s.at[4], z_r.at[4], aside)
    send(mine, a_at(0, 0), z_s.at[2], z_r.at[2], {"col": at_z(4 - step)})
    to_x(mine, 0, 0)
    to_x(theirs, 1, 0)
    to_twin(mine, 0)
    to_twin(theirs, 2)
    keep(mine, 0)

    def on_z(n):
        if n == 3:
            ref = b_at(row, layer, 1 - layer)
            arrived(ref, z_s.at[n], z_r.at[n])
            send(ref, a_at(0, 3), z_s.at[5], z_r.at[5], {"col": at_z(away)})
        else:
            ref = a_at(0, n)
            arrived(ref, z_s.at[n], z_r.at[n])
            if n == 1:
                pass_far(ref, 0)
            if n == 4:
                send(ref, ref, z_s.at[6], z_r.at[6], {"col": at_z(4 - away)})
        to_y(ref, n)
        if n == 3:
            to_x(ref, 0, 1)
            to_twin(ref, 1)
            keep(ref, 3)

    def on_y(n, k):
        d = (4 - sense(n), sense(n))[k]
        ref = a_at(d, n)
        arrived(ref, y_s.at[n, k], y_r.at[n, k])
        if n == 1:
            pass_far(ref, 1 + k)
        if k == 0:
            send(ref, ref, f_s.at[n], f_r.at[n], {"col": at_y(sense(n))})

    def on_f(n):
        ref = a_at(2, n)
        arrived(ref, f_s.at[n], f_r.at[n])
        if n == 1:
            pass_far(ref, 3)

    def on_far(m):
        arrived(a_at((0, 4 - sense(1), sense(1), 2)[m], 7), g_s.at[m], g_r.at[m])

    def on_x(d, h, own):
        there = ((x + XS - d) % XS) * 2 + core
        ref = b_at(there, (layer, 1 - layer)[h], (layer, 1 - layer)[own])
        n = h * 2 + own
        arrived(ref, x_s.at[n, d - 1], x_r.at[n, d - 1])
        to_twin(ref, 4 + n * 3 + d - 1)

    on_z(3)
    on_z(1)
    on_y(0, 0)
    on_z(4)
    send(mine, mine, e_s, e_r, other)
    on_y(0, 1)
    on_y(3, 0)
    on_y(1, 0)
    on_y(1, 1)
    on_z(2)
    for d in (1, 3):
        on_x(d, 0, 0)
    on_y(4, 0)
    on_f(1)
    on_z(5)
    on_z(6)
    for d in (1, 3):
        on_x(d, 1, 0)
    ref = b_at(row, 1 - layer, 1 - layer)
    arrived(ref, e_s, e_r)
    to_x(ref, 1, 1)
    to_twin(ref, 3)
    on_y(2, 0)
    on_x(2, 0, 0)
    on_x(2, 1, 0)
    on_y(5, 0)
    for d in (1, 3, 2):
        on_x(d, 0, 1)
    on_y(6, 0)
    for d in (1, 3, 2):
        on_x(d, 1, 1)
    for n in (3, 4, 2, 5, 6):
        on_y(n, 1)
    for n in (0, 3, 4, 2, 5, 6):
        on_f(n)
    for m in range(4):
        on_far(m)
    for n in range(4):
        h, s = (layer, 1 - layer)[n // 2], (layer, 1 - layer)[n % 2]
        arrived(b_at(twin, h, s), t_s.at[n], t_r.at[n])
        for d in (1, 2, 3):
            there = ((x + XS - d) % XS) * 2 + 1 - core
            m = 4 + n * 3 + d - 1
            arrived(b_at(there, h, s), t_s.at[m], t_r.at[m])
    for copy in sends:
        copy.wait_send()
    for copy in local:
        copy.wait()


def gather(d, p):
    wide = jax.ShapeDtypeStruct((TILES, 2, UNIT, W), BF16)
    dma = pltpu.SemaphoreType.DMA
    return pl.pallas_call(
        gather_kernel,
        out_shape=(wide, wide),
        in_specs=[pl.BlockSpec(memory_space=pltpu.VMEM)] * 2,
        out_specs=(pl.BlockSpec(memory_space=pltpu.VMEM),) * 2,
        scratch_shapes=[
            dma, dma,
            dma((7,)), dma((7,)),
            dma((7, 2)), dma((7, 2)),
            dma((7,)), dma((7,)),
            dma((4,)), dma((4,)),
            dma((4, 3)), dma((4, 3)),
            dma((16,)), dma((16,)),
            dma((2,)),
        ],
        compiler_params=pltpu.CompilerParams(
            collective_id=0, has_side_effects=True, vmem_limit_bytes=30 << 20
        ),
        name="gather",
    )(d, p)


CHUNK = W
MOST = TILES * 2 * HALF


def turn(v):
    return jnp.concatenate([v[:, B:], v[:, :B]], axis=1)


def pattern(ref, t):
    one = ref[t, 0, pl.ds(BODY, PAIRS), :].astype(F32)
    two = ref[t, 1, pl.ds(BODY, PAIRS), :].astype(F32)
    near = lanes(PAIRS) < B
    return jnp.concatenate([jnp.where(near, one, turn(two)), jnp.where(near, turn(one), two)], axis=0)


def in_row(block):
    sub = lax.broadcasted_iota(jnp.int32, (HALF, W), 0)
    return jnp.sum(jnp.where(lanes(HALF) % B == sub, block, 0.0), axis=0, keepdims=True)


def match(a_ref, b_ref, codes, t, want):
    want_turned = turn(want)
    right = lanes(1) >= B
    used = lanes(1) % B < HALF
    inner = in_row(pattern(a_ref, t))
    table = pattern(b_ref, t)
    hot = inner == lax.broadcasted_iota(jnp.int32, (HALF, W), 0).astype(F32)
    own = jnp.sum(jnp.where(hot, table, 0.0), axis=0, keepdims=True)
    other = jnp.sum(jnp.where(hot, turn(table), 0.0), axis=0, keepdims=True)
    live = used & (inner >= 0)

    def same(u, v):
        return jnp.where(live & (u == v) & (v >= 0), 1, 0)

    f0, f1 = same(own, want), same(other, want)
    f2, f3 = same(own, want_turned), same(other, want_turned)
    flags = (
        jnp.where(right, f3, f0) + 2 * jnp.where(right, f0, f3)
        + 4 * jnp.where(right, f2, f1) + 8 * jnp.where(right, f1, f2)
    )
    place = lanes(1) % B + jnp.where(right, HALF, 0) + t * 2 * HALF
    codes[pl.ds(t, 1), :] = jnp.where(flags > 0, flags + 16 * inner.astype(jnp.int32) + 512 * place, 0)


def multiply_kernel(a_ref, b_ref, o_ref, acc, codes, ranks, hits, listed, total, counts, sem):
    col = lax.axis_index("col")
    want = in_row(pattern(a_ref, col))
    for t in range(TILES):
        match(a_ref, b_ref, codes, t, want)

    code = codes[...]
    hit = jnp.where(code > 0, 1.0, 0.0).astype(BF16)
    down = lax.broadcasted_iota(jnp.int32, (W, W), 0)
    before = jnp.where(down < lanes(W), 1.0, 0.0).astype(BF16)
    in_tile = jnp.dot(hit, before, preferred_element_type=F32)
    of_tile = jnp.dot(hit, jnp.ones((W, W), BF16), preferred_element_type=F32)
    tiles = lax.broadcasted_iota(jnp.int32, (TILES, TILES), 0)
    above = jnp.where(lax.broadcasted_iota(jnp.int32, (TILES, TILES), 1) < tiles, 1.0, 0.0).astype(BF16)
    rank = in_tile + jnp.dot(above, of_tile.astype(BF16), preferred_element_type=F32)
    ranks[...] = jnp.where(code > 0, rank, -1.0)
    total[...] = jnp.broadcast_to(jnp.sum(of_tile, axis=0, keepdims=True).astype(jnp.int32), (8, W))
    count = pltpu.make_async_copy(total, counts, sem)
    count.start()

    @pl.loop(0, HALF)
    def _(j):
        acc[j] = jnp.zeros((B, W), F32)

    count.wait()
    number = counts[0, 0]

    @pl.loop(0, MOST // CHUNK)
    def _(c):
        @pl.when(c * CHUNK < number)
        def _():
            wanted = (down + c * CHUNK).astype(F32)
            found = jnp.zeros((CHUNK, W), F32)
            for t in range(TILES):
                value = codes[pl.ds(t, 1), :].astype(F32)
                found += jnp.where(ranks[pl.ds(t, 1), :] == wanted, value, 0.0)
            column = jnp.sum(found, axis=1, keepdims=True)
            line = jnp.sum(jnp.where(down == lanes(W), column, 0.0), axis=0, keepdims=True)
            hits[...] = jnp.broadcast_to(line.astype(jnp.int32), (8, W))
            copy = pltpu.make_async_copy(hits, listed, sem)
            copy.start()
            copy.wait()

            @pl.loop(0, (jnp.minimum(number - c * CHUNK, CHUNK) + 3) // 4)
            def _(n):
                products = []
                for m in range(4):
                    code = listed[0, n * 4 + m]
                    k, place = (code // 16) % HALF, code // 512
                    t, s, j = place // (2 * HALF), (place // HALF) % 2, place % HALF
                    at = pl.ds(pl.multiple_of(k % PAIRS * B, B), B)
                    from_row = pl.ds(pl.multiple_of(j % PAIRS * B, B), B)
                    far, q = k // PAIRS, j // PAIRS
                    near = lanes(1) < B

                    def pick(bit_left, bit_right):
                        return jnp.where(near, (code // bit_left) % 2, (code // bit_right) % 2).astype(F32)

                    one, two = b_ref[t, 0, at, :].astype(F32), b_ref[t, 1, at, :].astype(F32)
                    v = jnp.where(
                        far == 1,
                        jnp.where(near, turn(one), two),
                        jnp.where(near, one, turn(two)),
                    )
                    w = (v * pick(1, 2) + turn(v) * pick(4, 8)).astype(BF16)
                    a = a_ref[t, s, from_row, :]
                    a = a * jnp.where(lanes(1) // B == q, 1.0, 0.0).astype(BF16)
                    both = jnp.concatenate([w, w], axis=0)
                    products.append((j, jnp.dot(a, both, preferred_element_type=F32)))
                for j, product in products:
                    acc[j] += product

    left = lanes(1) < B

    @pl.loop(0, PAIRS)
    def _(j):
        at = pl.ds(pl.multiple_of(j * B, B), B)
        one, two = a_ref[col, 0, at, :].astype(F32), a_ref[col, 1, at, :].astype(F32)
        for q in (0, 1):
            full = acc[q * PAIRS + j]
            mine = jnp.where(left, one, turn(two)) if q == 0 else jnp.where(left, turn(one), two)
            raised = 2.0 * mine - full
            o_ref[0, q * PAIRS + j] = jnp.where(left, full, turn(raised)).astype(BF16)
            o_ref[1, q * PAIRS + j] = jnp.where(left, turn(full), raised).astype(BF16)


def multiply(a, b):
    return pl.pallas_call(
        multiply_kernel,
        out_shape=jax.ShapeDtypeStruct((2, HALF, B, W), BF16),
        in_specs=[pl.BlockSpec(memory_space=pltpu.VMEM)] * 2,
        out_specs=pl.BlockSpec(memory_space=pltpu.VMEM),
        scratch_shapes=[
            pltpu.VMEM((HALF, B, W), F32),
            pltpu.VMEM((TILES, W), jnp.int32),
            pltpu.VMEM((TILES, W), F32),
            pltpu.VMEM((8, W), jnp.int32),
            pltpu.SMEM((8, W), jnp.int32),
            pltpu.VMEM((8, W), jnp.int32),
            pltpu.SMEM((8, W), jnp.int32),
            pltpu.SemaphoreType.DMA,
        ],
        compiler_params=pltpu.CompilerParams(vmem_limit_bytes=32 << 20),
        name="multiply",
    )(a, b)


CUTS = 4


def swap_kernel(o_ref, sq_ref, ra_ref, got, s_sem, r_sem):
    layer = lax.axis_index("layer")
    other = {"layer": 1 - layer}
    barrier = pltpu.get_barrier_semaphore()
    pl.semaphore_signal(barrier, inc=1, device_id=other, device_id_type=MESH)
    pl.semaphore_wait(barrier, 1)
    size = HALF // CUTS
    copies = []
    for n in range(CUTS):
        at = pl.ds(n * size, size)
        copy = pltpu.make_async_remote_copy(
            src_ref=o_ref.at[1 - layer, at], dst_ref=got.at[at], send_sem=s_sem.at[n], recv_sem=r_sem.at[n],
            device_id=other, device_id_type=MESH,
        )
        copy.start()
        copies.append(copy)

    @pl.loop(0, HALF)
    def _(j):
        both = o_ref[layer, j]
        sq_ref[layer * HALF + j] = both[:, :B]
        ra_ref[layer * HALF + j] = both[:, B:]

    for n, copy in enumerate(copies):
        copy.wait_recv()

        @pl.loop(n * size, (n + 1) * size)
        def _(j):
            both = got[j]
            sq_ref[(1 - layer) * HALF + j] = both[:, :B]
            ra_ref[(1 - layer) * HALF + j] = both[:, B:]

    for copy in copies:
        copy.wait_send()


def swap(o):
    out = jax.ShapeDtypeStruct((2 * HALF, B, B), BF16)
    return pl.pallas_call(
        swap_kernel,
        out_shape=(out, out),
        in_specs=[pl.BlockSpec(memory_space=pltpu.VMEM)],
        out_specs=(pl.BlockSpec(memory_space=pltpu.VMEM),) * 2,
        scratch_shapes=[
            pltpu.VMEM((HALF, B, W), BF16),
            pltpu.SemaphoreType.DMA((CUTS,)),
            pltpu.SemaphoreType.DMA((CUTS,)),
        ],
        compiler_params=pltpu.CompilerParams(
            collective_id=1, has_side_effects=True, vmem_limit_bytes=12 << 20
        ),
        name="swap",
    )(o)


def on_device(density, pattern):
    a, b = gather(density.reshape(2 * HALF, B, B), pattern.reshape(1, 2 * HALF))
    squared, raised = swap(multiply(a, b))
    return squared.reshape(density.shape), raised.reshape(density.shape)


def solution(mesh):
    placed = (P("row", "col", "layer", None, None), P("row", "col", "layer"))
    return jax.shard_map(
        on_device,
        mesh=mesh,
        in_specs=placed,
        out_specs=(P("row", "col", "layer", None, None), P("row", "col", "layer", None, None)),
        check_vma=False,
    )
```

```python
import jax
import jax.numpy as jnp
from jax import lax
from jax.experimental import pallas as pl
from jax.experimental.pallas import tpu as pltpu
from jax.sharding import PartitionSpec as P

MESH = pl.DeviceIdType.MESH
F32 = jnp.float32
BF16 = jnp.bfloat16

B = 64
W = 2 * B
HALF = 32
PAIRS = HALF // 2
BODY = PAIRS * B
UNIT = BODY + PAIRS
TILES = 16
YS, ZS, XS = 4, 4, 4


def lanes(rows):
    return lax.broadcasted_iota(jnp.int32, (rows, W), 1)


def gather_kernel(d_ref, p_ref, a_ref, b_ref,
                  e_s, e_r, z_s, z_r, y_s, y_r, f_s, f_r, g_s, g_r, x_s, x_r, t_s, t_r, l_s):
    layer, row, col = lax.axis_index("layer"), lax.axis_index("row"), lax.axis_index("col")
    x, core = row // 2, row % 2
    y, z = col // ZS, col % ZS
    twin = x * 2 + 1 - core
    step, away = 1 + 2 * core, 3 - 2 * layer

    def at_z(d):
        return y * ZS + (z + d) % ZS

    def at_y(d):
        return ((y + d) % YS) * ZS + z

    def at_x(d):
        return ((x + d) % XS) * 2 + core

    other = {"layer": 1 - layer}
    aside = {"layer": 1 - layer, "col": at_z(away)}
    peers = [other, aside, {"row": twin}]
    peers += [{"col": at_z(d)} for d in (1, 3)]
    peers += [{"col": at_y(d)} for d in (1, 3)]
    peers += [{"row": at_x(d)} for d in (1, 2, 3)]
    barrier = pltpu.get_barrier_semaphore()
    for peer in peers:
        pl.semaphore_signal(barrier, inc=1, device_id=peer, device_id_type=MESH)

    number = p_ref[...].astype(F32)
    lane = lax.broadcasted_iota(jnp.int32, (PAIRS, B), 1)
    sub = lax.broadcasted_iota(jnp.int32, (PAIRS, B), 0)

    def entry(first):
        return jnp.sum(jnp.where(lane == sub + first, number, 0.0), axis=1, keepdims=True)

    for h in (0, 1):
        @pl.loop(0, PAIRS)
        def _(j):
            b_ref[2 * row + h, layer, pl.ds(pl.multiple_of(j * B, B), B), :] = jnp.concatenate(
                [d_ref[h * HALF + j], d_ref[h * HALF + PAIRS + j]], axis=1
            )

        b_ref[2 * row + h, layer, pl.ds(BODY, PAIRS), :] = jnp.where(
            lanes(PAIRS) < B, entry(h * HALF), entry(h * HALF + PAIRS)
        ).astype(BF16)

    pl.semaphore_wait(barrier, len(peers))

    sends, local = [], []

    def send(src, dst, ssem, rsem, peer):
        copy = pltpu.make_async_remote_copy(
            src_ref=src, dst_ref=dst, send_sem=ssem, recv_sem=rsem, device_id=peer, device_id_type=MESH
        )
        copy.start()
        sends.append(copy)

    def arrived(ref, ssem, rsem):
        pltpu.make_async_remote_copy(
            src_ref=ref, dst_ref=ref, send_sem=ssem, recv_sem=rsem, device_id=other, device_id_type=MESH
        ).wait_recv()

    offset = (0, 4 - step, step, 0, away, 4 - away, 2, 2)
    whose = (layer, layer, layer, 1 - layer, 1 - layer, 1 - layer, 1 - layer, layer)

    def a_at(dy, n):
        return a_ref.at[((y + dy) % YS) * ZS + (z + offset[n]) % ZS, whose[n]]

    def b_at(there, h, s):
        return b_ref.at[2 * there + h, s]

    mine, theirs = b_at(row, layer, layer), b_at(row, 1 - layer, layer)

    def sense(n):
        return 1 + 2 * ((n + core) % 2)

    def to_y(src, n):
        for k, d in enumerate((sense(n), 4 - sense(n))):
            send(src, a_at(0, n), y_s.at[n, k], y_r.at[n, k], {"col": at_y(d)})

    def to_x(src, h, own):
        n = h * 2 + own
        for d in (1, 3, 2):
            send(src, src, x_s.at[n, d - 1], x_r.at[n, d - 1], {"row": at_x(d)})

    def to_twin(src, n):
        send(src, src, t_s.at[n], t_r.at[n], {"row": twin})

    def keep(src, n):
        copy = pltpu.make_async_copy(src, a_at(0, n), l_s.at[n // 3])
        copy.start()
        local.append(copy)

    def pass_far(ref, m):
        send(ref, ref, g_s.at[m], g_r.at[m], {"col": at_z(step)})

    to_y(mine, 0)
    send(theirs, theirs, z_s.at[3], z_r.at[3], other)
    send(mine, a_at(0, 0), z_s.at[1], z_r.at[1], {"col": at_z(step)})
    send(theirs, a_at(0, 0), z_s.at[4], z_r.at[4], aside)
    send(mine, a_at(0, 0), z_s.at[2], z_r.at[2], {"col": at_z(4 - step)})
    to_x(mine, 0, 0)
    to_x(theirs, 1, 0)
    to_twin(mine, 0)
    to_twin(theirs, 2)
    keep(mine, 0)

    def on_z(n):
        if n == 3:
            ref = b_at(row, layer, 1 - layer)
            arrived(ref, z_s.at[n], z_r.at[n])
            send(ref, a_at(0, 3), z_s.at[5], z_r.at[5], {"col": at_z(away)})
        else:
            ref = a_at(0, n)
            arrived(ref, z_s.at[n], z_r.at[n])
            if n == 1:
                pass_far(ref, 0)
            if n == 4:
                send(ref, ref, z_s.at[6], z_r.at[6], {"col": at_z(4 - away)})
        to_y(ref, n)
        if n == 3:
            to_x(ref, 0, 1)
            to_twin(ref, 1)
            keep(ref, 3)

    def on_y(n, k):
        d = (4 - sense(n), sense(n))[k]
        ref = a_at(d, n)
        arrived(ref, y_s.at[n, k], y_r.at[n, k])
        if n == 1:
            pass_far(ref, 1 + k)
        if k == 0:
            send(ref, ref, f_s.at[n], f_r.at[n], {"col": at_y(sense(n))})

    def on_f(n):
        ref = a_at(2, n)
        arrived(ref, f_s.at[n], f_r.at[n])
        if n == 1:
            pass_far(ref, 3)

    def on_far(m):
        arrived(a_at((0, 4 - sense(1), sense(1), 2)[m], 7), g_s.at[m], g_r.at[m])

    def on_x(d, h, own):
        there = ((x + XS - d) % XS) * 2 + core
        ref = b_at(there, (layer, 1 - layer)[h], (layer, 1 - layer)[own])
        n = h * 2 + own
        arrived(ref, x_s.at[n, d - 1], x_r.at[n, d - 1])
        to_twin(ref, 4 + n * 3 + d - 1)

    on_z(3)
    on_z(1)
    on_y(0, 0)
    on_z(4)
    send(mine, mine, e_s, e_r, other)
    on_y(0, 1)
    on_y(3, 0)
    on_y(1, 0)
    on_y(1, 1)
    on_z(2)
    for d in (1, 3):
        on_x(d, 0, 0)
    on_y(4, 0)
    on_f(1)
    on_z(5)
    on_z(6)
    for d in (1, 3):
        on_x(d, 1, 0)
    ref = b_at(row, 1 - layer, 1 - layer)
    arrived(ref, e_s, e_r)
    to_x(ref, 1, 1)
    to_twin(ref, 3)
    on_y(2, 0)
    on_x(2, 0, 0)
    on_x(2, 1, 0)
    on_y(5, 0)
    for d in (1, 3, 2):
        on_x(d, 0, 1)
    on_y(6, 0)
    for d in (1, 3, 2):
        on_x(d, 1, 1)
    for n in (3, 4, 2, 5, 6):
        on_y(n, 1)
    for n in (0, 3, 4, 2, 5, 6):
        on_f(n)
    for m in range(4):
        on_far(m)
    for n in range(4):
        h, s = (layer, 1 - layer)[n // 2], (layer, 1 - layer)[n % 2]
        arrived(b_at(twin, h, s), t_s.at[n], t_r.at[n])
        for d in (1, 2, 3):
            there = ((x + XS - d) % XS) * 2 + 1 - core
            m = 4 + n * 3 + d - 1
            arrived(b_at(there, h, s), t_s.at[m], t_r.at[m])
    for copy in sends:
        copy.wait_send()
    for copy in local:
        copy.wait()


def gather(d, p):
    wide = jax.ShapeDtypeStruct((TILES, 2, UNIT, W), BF16)
    dma = pltpu.SemaphoreType.DMA
    return pl.pallas_call(
        gather_kernel,
        out_shape=(wide, wide),
        in_specs=[pl.BlockSpec(memory_space=pltpu.VMEM)] * 2,
        out_specs=(pl.BlockSpec(memory_space=pltpu.VMEM),) * 2,
        scratch_shapes=[
            dma, dma,
            dma((7,)), dma((7,)),
            dma((7, 2)), dma((7, 2)),
            dma((7,)), dma((7,)),
            dma((4,)), dma((4,)),
            dma((4, 3)), dma((4, 3)),
            dma((16,)), dma((16,)),
            dma((2,)),
        ],
        compiler_params=pltpu.CompilerParams(
            collective_id=0, has_side_effects=True, vmem_limit_bytes=30 << 20
        ),
        name="gather",
    )(d, p)


CHUNK = W
MOST = TILES * 2 * HALF


def turn(v):
    return jnp.concatenate([v[:, B:], v[:, :B]], axis=1)


def pattern(ref, t):
    one = ref[t, 0, pl.ds(BODY, PAIRS), :].astype(F32)
    two = ref[t, 1, pl.ds(BODY, PAIRS), :].astype(F32)
    near = lanes(PAIRS) < B
    return jnp.concatenate([jnp.where(near, one, turn(two)), jnp.where(near, turn(one), two)], axis=0)


def in_row(block):
    sub = lax.broadcasted_iota(jnp.int32, (HALF, W), 0)
    return jnp.sum(jnp.where(lanes(HALF) % B == sub, block, 0.0), axis=0, keepdims=True)


def match(a_ref, b_ref, codes, t, want):
    want_turned = turn(want)
    right = lanes(1) >= B
    used = lanes(1) % B < HALF
    inner = in_row(pattern(a_ref, t))
    table = pattern(b_ref, t)
    hot = inner == lax.broadcasted_iota(jnp.int32, (HALF, W), 0).astype(F32)
    own = jnp.sum(jnp.where(hot, table, 0.0), axis=0, keepdims=True)
    other = jnp.sum(jnp.where(hot, turn(table), 0.0), axis=0, keepdims=True)
    live = used & (inner >= 0)

    def same(u, v):
        return jnp.where(live & (u == v) & (v >= 0), 1, 0)

    f0, f1 = same(own, want), same(other, want)
    f2, f3 = same(own, want_turned), same(other, want_turned)
    flags = (
        jnp.where(right, f3, f0) + 2 * jnp.where(right, f0, f3)
        + 4 * jnp.where(right, f2, f1) + 8 * jnp.where(right, f1, f2)
    )
    place = lanes(1) % B + jnp.where(right, HALF, 0) + t * 2 * HALF
    codes[pl.ds(t, 1), :] = jnp.where(flags > 0, flags + 16 * inner.astype(jnp.int32) + 512 * place, 0)


GROUP = 8


def multiply_kernel(a_ref, b_ref, acc, codes, ranks, hits, listed, sem):
    col = lax.axis_index("col")
    want = in_row(pattern(a_ref, col))
    for t in range(TILES):
        match(a_ref, b_ref, codes, t, want)

    code = codes[...]
    hit = jnp.where(code > 0, 1.0, 0.0).astype(BF16)
    down = lax.broadcasted_iota(jnp.int32, (W, W), 0)
    before = jnp.where(down < lanes(W), 1.0, 0.0).astype(BF16)
    in_tile = jnp.dot(hit, before, preferred_element_type=F32)
    of_tile = jnp.dot(hit, jnp.ones((W, W), BF16), preferred_element_type=F32)
    tiles = lax.broadcasted_iota(jnp.int32, (TILES, TILES), 0)
    above = jnp.where(lax.broadcasted_iota(jnp.int32, (TILES, TILES), 1) < tiles, 1.0, 0.0).astype(BF16)
    rank = in_tile + jnp.dot(above, of_tile.astype(BF16), preferred_element_type=F32)
    ranks[...] = jnp.where(code > 0, rank, -1.0)
    total = jnp.sum(of_tile, axis=0, keepdims=True).astype(jnp.int32)
    hits[...] = jnp.broadcast_to(total, (8, W))

    def enlist(c):
        wanted = (down + c * CHUNK).astype(F32)
        found = jnp.zeros((CHUNK, W), F32)
        for t in range(TILES):
            found += jnp.where(ranks[pl.ds(t, 1), :] == wanted, codes[pl.ds(t, 1), :].astype(F32), 0.0)
        column = jnp.sum(found, axis=1, keepdims=True)
        line = jnp.sum(jnp.where(down == lanes(W), column, 0.0), axis=0, keepdims=True)
        hits[pl.ds(0, 1), :] = line.astype(jnp.int32)
        copy = pltpu.make_async_copy(hits, listed, sem)
        copy.start()
        return copy

    def product(code):
        k, place = (code // 16) % HALF, code // 512
        t, s, j = place // (2 * HALF), (place // HALF) % 2, place % HALF
        at = pl.ds(pl.multiple_of(k % PAIRS * B, B), B)
        from_row = pl.ds(pl.multiple_of(j % PAIRS * B, B), B)
        far, q = k // PAIRS, j // PAIRS
        near = lanes(1) < B

        def pick(bit_left, bit_right):
            return jnp.where(near, (code // bit_left) % 2, (code // bit_right) % 2).astype(F32)

        stay = b_ref[t, far, at, :].astype(F32)
        move = b_ref[t, 1 - far, at, :].astype(F32)
        here = lanes(B) // B == far
        straight = jnp.where(here, stay, turn(move))
        crossed = jnp.where(here, move, turn(stay))
        w = (straight * pick(1, 2) + crossed * pick(4, 8)).astype(BF16)
        a = a_ref[t, s, from_row, :] * jnp.where(lanes(1) // B == q, 1.0, 0.0).astype(BF16)
        return j, jnp.dot(a, jnp.concatenate([w, w], axis=0), preferred_element_type=F32)

    def run(number):
        @pl.loop(0, (number + GROUP - 1) // GROUP)
        def _(n):
            for j, value in [product(listed[0, n * GROUP + m]) for m in range(GROUP)]:
                acc[j] += value

    first = enlist(0)

    @pl.loop(0, HALF)
    def _(j):
        acc[j] = jnp.zeros((B, W), F32)

    first.wait()
    number = listed[1, 0]
    run(jnp.minimum(number, CHUNK))

    @pl.loop(1, MOST // CHUNK)
    def _(c):
        @pl.when(c * CHUNK < number)
        def _():
            enlist(c).wait()
            run(jnp.minimum(number - c * CHUNK, CHUNK))


def multiply(a, b):
    return pl.pallas_call(
        multiply_kernel,
        out_shape=jax.ShapeDtypeStruct((HALF, B, W), F32),
        in_specs=[pl.BlockSpec(memory_space=pltpu.VMEM)] * 2,
        out_specs=pl.BlockSpec(memory_space=pltpu.VMEM),
        scratch_shapes=[
            pltpu.VMEM((TILES, W), jnp.int32),
            pltpu.VMEM((TILES, W), F32),
            pltpu.VMEM((8, W), jnp.int32),
            pltpu.SMEM((8, W), jnp.int32),
            pltpu.SemaphoreType.DMA,
        ],
        compiler_params=pltpu.CompilerParams(vmem_limit_bytes=32 << 20),
        name="multiply",
    )(a, b)


CUTS = 4


def swap_kernel(acc, a_ref, sq_ref, ra_ref, out, got, s_sem, r_sem):
    layer, col = lax.axis_index("layer"), lax.axis_index("col")
    other = {"layer": 1 - layer}
    barrier = pltpu.get_barrier_semaphore()
    pl.semaphore_signal(barrier, inc=1, device_id=other, device_id_type=MESH)
    size = HALF // CUTS
    near = lanes(1) < B

    def finish(n):
        @pl.loop(n * size // 2, (n + 1) * size // 2)
        def _(j):
            at = pl.ds(pl.multiple_of(j * B, B), B)
            one, two = a_ref[col, 0, at, :].astype(F32), a_ref[col, 1, at, :].astype(F32)
            for q in (0, 1):
                full = acc[q * PAIRS + j]
                mine = jnp.where(near, one, turn(two)) if q == 0 else jnp.where(near, turn(one), two)
                raised = 2.0 * mine - full
                out[0, 2 * j + q] = jnp.where(near, full, turn(raised)).astype(BF16)
                out[1, 2 * j + q] = jnp.where(near, turn(full), raised).astype(BF16)

    def unpack(both, half, n):
        @pl.loop(n * size // 2, (n + 1) * size // 2)
        def _(j):
            for q in (0, 1):
                v = both[2 * j + q]
                sq_ref[half * HALF + q * PAIRS + j] = v[:, :B]
                ra_ref[half * HALF + q * PAIRS + j] = v[:, B:]

    copies = []
    for n in range(CUTS):
        finish(n)
        if n == 0:
            pl.semaphore_wait(barrier, 1)
        at = pl.ds(n * size, size)
        copy = pltpu.make_async_remote_copy(
            src_ref=out.at[1 - layer, at], dst_ref=got.at[at], send_sem=s_sem.at[n], recv_sem=r_sem.at[n],
            device_id=other, device_id_type=MESH,
        )
        copy.start()
        copies.append(copy)
    for n in range(CUTS):
        unpack(out.at[layer], layer, n)
    for n, copy in enumerate(copies):
        copy.wait_recv()
        unpack(got, 1 - layer, n)
    for copy in copies:
        copy.wait_send()


def swap(acc, a):
    out = jax.ShapeDtypeStruct((2 * HALF, B, B), BF16)
    return pl.pallas_call(
        swap_kernel,
        out_shape=(out, out),
        in_specs=[pl.BlockSpec(memory_space=pltpu.VMEM)] * 2,
        out_specs=(pl.BlockSpec(memory_space=pltpu.VMEM),) * 2,
        scratch_shapes=[
            pltpu.VMEM((2, HALF, B, W), BF16),
            pltpu.VMEM((HALF, B, W), BF16),
            pltpu.SemaphoreType.DMA((CUTS,)),
            pltpu.SemaphoreType.DMA((CUTS,)),
        ],
        compiler_params=pltpu.CompilerParams(
            collective_id=1, has_side_effects=True, vmem_limit_bytes=24 << 20
        ),
        name="swap",
    )(acc, a)


def on_device(density, pattern):
    a, b = gather(density.reshape(2 * HALF, B, B), pattern.reshape(1, 2 * HALF))
    squared, raised = swap(multiply(a, b), a)
    return squared.reshape(density.shape), raised.reshape(density.shape)


def solution(mesh):
    placed = (P("row", "col", "layer", None, None), P("row", "col", "layer"))
    return jax.shard_map(
        on_device,
        mesh=mesh,
        in_specs=placed,
        out_specs=(P("row", "col", "layer", None, None), P("row", "col", "layer", None, None)),
        check_vma=False,
    )
```

```python
import jax
import jax.numpy as jnp
from jax import lax
from jax.experimental import pallas as pl
from jax.experimental.pallas import tpu as pltpu
from jax.sharding import PartitionSpec as P

MESH = pl.DeviceIdType.MESH
F32 = jnp.float32
BF16 = jnp.bfloat16

B = 64
W = 2 * B
HALF = 32
PAIRS = HALF // 2
BODY = PAIRS * B
UNIT = BODY + PAIRS
TILES = 16
CUT = (0, 528, 1040)
PIECES = range(len(CUT) - 1)
YS, ZS, XS = 4, 4, 4


def lanes(rows):
    return lax.broadcasted_iota(jnp.int32, (rows, W), 1)


def gather_kernel(d_ref, p_ref, a_ref, b_ref,
                  e_s, e_r, z_s, z_r, y_s, y_r, f_s, f_r, g_s, g_r, x_s, x_r, t_s, t_r, l_s):
    layer, row, col = lax.axis_index("layer"), lax.axis_index("row"), lax.axis_index("col")
    x, core = row // 2, row % 2
    y, z = col // ZS, col % ZS
    twin = x * 2 + 1 - core
    step, away = 1 + 2 * core, 3 - 2 * layer

    def at_z(d):
        return y * ZS + (z + d) % ZS

    def at_y(d):
        return ((y + d) % YS) * ZS + z

    def at_x(d):
        return ((x + d) % XS) * 2 + core

    other = {"layer": 1 - layer}
    aside = {"layer": 1 - layer, "col": at_z(away)}
    peers = [other, aside, {"row": twin}]
    peers += [{"col": at_z(d)} for d in (1, 3)]
    peers += [{"col": at_y(d)} for d in (1, 3)]
    peers += [{"row": at_x(d)} for d in (1, 2, 3)]
    barrier = pltpu.get_barrier_semaphore()
    for peer in peers:
        pl.semaphore_signal(barrier, inc=1, device_id=peer, device_id_type=MESH)

    number = p_ref[...].astype(F32)
    lane = lax.broadcasted_iota(jnp.int32, (PAIRS, B), 1)
    sub = lax.broadcasted_iota(jnp.int32, (PAIRS, B), 0)

    def entry(first):
        return jnp.sum(jnp.where(lane == sub + first, number, 0.0), axis=1, keepdims=True)

    for h in (0, 1):
        @pl.loop(0, PAIRS)
        def _(j):
            b_ref[2 * row + h, layer, pl.ds(pl.multiple_of(j * B, B), B), :] = jnp.concatenate(
                [d_ref[h * HALF + j], d_ref[h * HALF + PAIRS + j]], axis=1
            )

        b_ref[2 * row + h, layer, pl.ds(BODY, PAIRS), :] = jnp.where(
            lanes(PAIRS) < B, entry(h * HALF), entry(h * HALF + PAIRS)
        ).astype(BF16)

    pl.semaphore_wait(barrier, len(peers))

    sends, local = [], []

    def send(src, dst, ssem, rsem, peer):
        copy = pltpu.make_async_remote_copy(
            src_ref=src, dst_ref=dst, send_sem=ssem, recv_sem=rsem, device_id=peer, device_id_type=MESH
        )
        copy.start()
        sends.append(copy)

    def arrived(ref, ssem, rsem):
        pltpu.make_async_remote_copy(
            src_ref=ref, dst_ref=ref, send_sem=ssem, recv_sem=rsem, device_id=other, device_id_type=MESH
        ).wait_recv()

    offset = (0, 4 - step, step, 0, away, 4 - away, 2, 2)
    whose = (layer, layer, layer, 1 - layer, 1 - layer, 1 - layer, 1 - layer, layer)

    def a_at(dy, n):
        return a_ref.at[((y + dy) % YS) * ZS + (z + offset[n]) % ZS, whose[n]]

    def b_at(there, h, s):
        return b_ref.at[2 * there + h, s]

    mine, theirs = b_at(row, layer, layer), b_at(row, 1 - layer, layer)

    def sense(n):
        return 1 + 2 * ((n + core) % 2)

    def piece(ref, p):
        return ref.at[pl.ds(CUT[p], CUT[p + 1] - CUT[p])]

    def to_y(src, n, p):
        for k, d in enumerate((sense(n), 4 - sense(n))):
            send(piece(src, p), piece(a_at(0, n), p), y_s.at[n, k, p], y_r.at[n, k, p], {"col": at_y(d)})

    def to_x(src, h, own):
        n = h * 2 + own
        for d in (1, 3, 2):
            send(src, src, x_s.at[n, d - 1], x_r.at[n, d - 1], {"row": at_x(d)})

    def to_twin(src, n):
        send(src, src, t_s.at[n], t_r.at[n], {"row": twin})

    def keep(src, n):
        copy = pltpu.make_async_copy(src, a_at(0, n), l_s.at[n // 3])
        copy.start()
        local.append(copy)

    def to_z(src, dst, n, p, peer):
        send(piece(src, p), piece(dst, p), z_s.at[n, p], z_r.at[n, p], peer)

    def pass_far(ref, m, p):
        send(piece(ref, p), piece(ref, p), g_s.at[m, p], g_r.at[m, p], {"col": at_z(step)})

    for p in PIECES:
        to_y(mine, 0, p)
        to_z(theirs, theirs, 3, p, other)
        to_z(mine, a_at(0, 0), 1, p, {"col": at_z(step)})
        to_z(theirs, a_at(0, 0), 4, p, aside)
        to_z(mine, a_at(0, 0), 2, p, {"col": at_z(4 - step)})
    to_x(mine, 0, 0)
    to_x(theirs, 1, 0)
    to_twin(mine, 0)
    to_twin(theirs, 2)
    keep(mine, 0)

    def on_z(n, p):
        ref = b_at(row, layer, 1 - layer) if n == 3 else a_at(0, n)
        arrived(piece(ref, p), z_s.at[n, p], z_r.at[n, p])
        if n == 3:
            to_z(ref, a_at(0, 3), 5, p, {"col": at_z(away)})
        if n == 1:
            pass_far(ref, 0, p)
        if n == 4:
            to_z(ref, ref, 6, p, {"col": at_z(4 - away)})
        to_y(ref, n, p)

    def on_y(n, k, p):
        d = (4 - sense(n), sense(n))[k]
        ref = a_at(d, n)
        arrived(piece(ref, p), y_s.at[n, k, p], y_r.at[n, k, p])
        if n == 1:
            pass_far(ref, 1 + k, p)
        if k == 0:
            send(piece(ref, p), piece(ref, p), f_s.at[n, p], f_r.at[n, p], {"col": at_y(sense(n))})

    def on_f(n, p):
        ref = a_at(2, n)
        arrived(piece(ref, p), f_s.at[n, p], f_r.at[n, p])
        if n == 1:
            pass_far(ref, 3, p)

    def on_far(m, p):
        arrived(piece(a_at((0, 4 - sense(1), sense(1), 2)[m], 7), p), g_s.at[m, p], g_r.at[m, p])

    def on_x(d, h, own):
        there = ((x + XS - d) % XS) * 2 + core
        ref = b_at(there, (layer, 1 - layer)[h], (layer, 1 - layer)[own])
        n = h * 2 + own
        arrived(ref, x_s.at[n, d - 1], x_r.at[n, d - 1])
        to_twin(ref, 4 + n * 3 + d - 1)

    for p in PIECES:
        on_z(3, p)
        if p == PIECES[-1]:
            send(mine, mine, e_s, e_r, other)
        on_z(1, p)
        on_y(0, 0, p)
        on_z(4, p)
    ref = b_at(row, layer, 1 - layer)
    to_x(ref, 0, 1)
    to_twin(ref, 1)
    keep(ref, 3)
    for p in PIECES:
        on_y(3, 0, p)
        on_y(1, 0, p)
        on_y(1, 1, p)
        on_z(2, p)
    for d in (1, 3):
        on_x(d, 0, 0)
    for p in PIECES:
        on_y(4, 0, p)
        on_f(1, p)
        on_z(5, p)
        on_z(6, p)
    for d in (1, 3):
        on_x(d, 1, 0)
    ref = b_at(row, 1 - layer, 1 - layer)
    arrived(ref, e_s, e_r)
    to_x(ref, 1, 1)
    to_twin(ref, 3)
    for p in PIECES:
        on_y(2, 0, p)
    on_x(2, 0, 0)
    on_x(2, 1, 0)
    for p in PIECES:
        on_y(5, 0, p)
    for d in (1, 3, 2):
        on_x(d, 0, 1)
    for p in PIECES:
        on_y(6, 0, p)
    for d in (1, 3, 2):
        on_x(d, 1, 1)
    for p in PIECES:
        for n in (0, 3, 4, 2, 5, 6):
            on_y(n, 1, p)
            on_f(n, p)
        for m in range(4):
            on_far(m, p)
    for n in range(4):
        h, s = (layer, 1 - layer)[n // 2], (layer, 1 - layer)[n % 2]
        arrived(b_at(twin, h, s), t_s.at[n], t_r.at[n])
        for d in (1, 2, 3):
            there = ((x + XS - d) % XS) * 2 + 1 - core
            m = 4 + n * 3 + d - 1
            arrived(b_at(there, h, s), t_s.at[m], t_r.at[m])
    for copy in sends:
        copy.wait_send()
    for copy in local:
        copy.wait()


def gather(d, p):
    wide = jax.ShapeDtypeStruct((TILES, 2, UNIT, W), BF16)
    dma = pltpu.SemaphoreType.DMA
    return pl.pallas_call(
        gather_kernel,
        out_shape=(wide, wide),
        in_specs=[pl.BlockSpec(memory_space=pltpu.VMEM)] * 2,
        out_specs=(pl.BlockSpec(memory_space=pltpu.VMEM),) * 2,
        scratch_shapes=[
            dma, dma,
            dma((7, len(PIECES))), dma((7, len(PIECES))),
            dma((7, 2, len(PIECES))), dma((7, 2, len(PIECES))),
            dma((7, len(PIECES))), dma((7, len(PIECES))),
            dma((4, len(PIECES))), dma((4, len(PIECES))),
            dma((4, 3)), dma((4, 3)),
            dma((16,)), dma((16,)),
            dma((2,)),
        ],
        compiler_params=pltpu.CompilerParams(
            collective_id=0, has_side_effects=True, vmem_limit_bytes=30 << 20
        ),
        name="gather",
    )(d, p)


CHUNK = W
MOST = TILES * 2 * HALF


def turn(v):
    return jnp.concatenate([v[:, B:], v[:, :B]], axis=1)


def pattern(ref, t):
    one = ref[t, 0, pl.ds(BODY, PAIRS), :].astype(F32)
    two = ref[t, 1, pl.ds(BODY, PAIRS), :].astype(F32)
    near = lanes(PAIRS) < B
    return jnp.concatenate([jnp.where(near, one, turn(two)), jnp.where(near, turn(one), two)], axis=0)


def in_row(block):
    sub = lax.broadcasted_iota(jnp.int32, (HALF, W), 0)
    return jnp.sum(jnp.where(lanes(HALF) % B == sub, block, 0.0), axis=0, keepdims=True)


def match(a_ref, b_ref, codes, t, want):
    want_turned = turn(want)
    right = lanes(1) >= B
    used = lanes(1) % B < HALF
    inner = in_row(pattern(a_ref, t))
    table = pattern(b_ref, t)
    hot = inner == lax.broadcasted_iota(jnp.int32, (HALF, W), 0).astype(F32)
    own = jnp.sum(jnp.where(hot, table, 0.0), axis=0, keepdims=True)
    other = jnp.sum(jnp.where(hot, turn(table), 0.0), axis=0, keepdims=True)
    live = used & (inner >= 0)

    def same(u, v):
        return jnp.where(live & (u == v) & (v >= 0), 1, 0)

    f0, f1 = same(own, want), same(other, want)
    f2, f3 = same(own, want_turned), same(other, want_turned)
    flags = (
        jnp.where(right, f3, f0) + 2 * jnp.where(right, f0, f3)
        + 4 * jnp.where(right, f2, f1) + 8 * jnp.where(right, f1, f2)
    )
    place = lanes(1) % B + jnp.where(right, HALF, 0) + t * 2 * HALF
    codes[pl.ds(t, 1), :] = jnp.where(flags > 0, flags + 16 * inner.astype(jnp.int32) + 512 * place, 0)


GROUP = 8


def multiply_kernel(a_ref, b_ref, acc, codes, ranks, hits, listed, sem):
    col = lax.axis_index("col")
    want = in_row(pattern(a_ref, col))
    for t in range(TILES):
        match(a_ref, b_ref, codes, t, want)

    code = codes[...]
    hit = jnp.where(code > 0, 1.0, 0.0).astype(BF16)
    down = lax.broadcasted_iota(jnp.int32, (W, W), 0)
    before = jnp.where(down < lanes(W), 1.0, 0.0).astype(BF16)
    in_tile = jnp.dot(hit, before, preferred_element_type=F32)
    of_tile = jnp.dot(hit, jnp.ones((W, W), BF16), preferred_element_type=F32)
    tiles = lax.broadcasted_iota(jnp.int32, (TILES, TILES), 0)
    above = jnp.where(lax.broadcasted_iota(jnp.int32, (TILES, TILES), 1) < tiles, 1.0, 0.0).astype(BF16)
    rank = in_tile + jnp.dot(above, of_tile.astype(BF16), preferred_element_type=F32)
    ranks[...] = jnp.where(code > 0, rank, -1.0)
    total = jnp.sum(of_tile, axis=0, keepdims=True).astype(jnp.int32)
    hits[...] = jnp.broadcast_to(total, (8, W))

    def enlist(c):
        wanted = (down + c * CHUNK).astype(F32)
        found = jnp.zeros((CHUNK, W), F32)
        for t in range(TILES):
            found += jnp.where(ranks[pl.ds(t, 1), :] == wanted, codes[pl.ds(t, 1), :].astype(F32), 0.0)
        column = jnp.sum(found, axis=1, keepdims=True)
        line = jnp.sum(jnp.where(down == lanes(W), column, 0.0), axis=0, keepdims=True)
        hits[pl.ds(0, 1), :] = line.astype(jnp.int32)
        copy = pltpu.make_async_copy(hits, listed, sem)
        copy.start()
        return copy

    def product(code):
        k, place = (code // 16) % HALF, code // 512
        t, s, j = place // (2 * HALF), (place // HALF) % 2, place % HALF
        at = pl.ds(pl.multiple_of(k % PAIRS * B, B), B)
        from_row = pl.ds(pl.multiple_of(j % PAIRS * B, B), B)
        far, q = k // PAIRS, j // PAIRS
        near = lanes(1) < B

        def pick(bit_left, bit_right):
            return jnp.where(near, (code // bit_left) % 2, (code // bit_right) % 2).astype(F32)

        stay = b_ref[t, far, at, :].astype(F32)
        move = b_ref[t, 1 - far, at, :].astype(F32)
        here = lanes(B) // B == far
        straight = jnp.where(here, stay, turn(move))
        crossed = jnp.where(here, move, turn(stay))
        w = (straight * pick(1, 2) + crossed * pick(4, 8)).astype(BF16)
        a = a_ref[t, s, from_row, :] * jnp.where(lanes(1) // B == q, 1.0, 0.0).astype(BF16)
        return j, jnp.dot(a, jnp.concatenate([w, w], axis=0), preferred_element_type=F32)

    def run(number):
        @pl.loop(0, (number + GROUP - 1) // GROUP)
        def _(n):
            for j, value in [product(listed[0, n * GROUP + m]) for m in range(GROUP)]:
                acc[j] += value

    first = enlist(0)

    @pl.loop(0, HALF)
    def _(j):
        acc[j] = jnp.zeros((B, W), F32)

    first.wait()
    number = listed[1, 0]
    run(jnp.minimum(number, CHUNK))

    @pl.loop(1, MOST // CHUNK)
    def _(c):
        @pl.when(c * CHUNK < number)
        def _():
            enlist(c).wait()
            run(jnp.minimum(number - c * CHUNK, CHUNK))


def multiply(a, b):
    return pl.pallas_call(
        multiply_kernel,
        out_shape=jax.ShapeDtypeStruct((HALF, B, W), F32),
        in_specs=[pl.BlockSpec(memory_space=pltpu.VMEM)] * 2,
        out_specs=pl.BlockSpec(memory_space=pltpu.VMEM),
        scratch_shapes=[
            pltpu.VMEM((TILES, W), jnp.int32),
            pltpu.VMEM((TILES, W), F32),
            pltpu.VMEM((8, W), jnp.int32),
            pltpu.SMEM((8, W), jnp.int32),
            pltpu.SemaphoreType.DMA,
        ],
        compiler_params=pltpu.CompilerParams(vmem_limit_bytes=32 << 20),
        name="multiply",
    )(a, b)


CUTS = 4


def swap_kernel(acc, a_ref, sq_ref, ra_ref, out, got, s_sem, r_sem):
    layer, col = lax.axis_index("layer"), lax.axis_index("col")
    other = {"layer": 1 - layer}
    barrier = pltpu.get_barrier_semaphore()
    pl.semaphore_signal(barrier, inc=1, device_id=other, device_id_type=MESH)
    size = HALF // CUTS
    near = lanes(1) < B

    def finish(n):
        @pl.loop(n * size // 2, (n + 1) * size // 2)
        def _(j):
            at = pl.ds(pl.multiple_of(j * B, B), B)
            one, two = a_ref[col, 0, at, :].astype(F32), a_ref[col, 1, at, :].astype(F32)
            for q in (0, 1):
                full = acc[q * PAIRS + j]
                mine = jnp.where(near, one, turn(two)) if q == 0 else jnp.where(near, turn(one), two)
                raised = 2.0 * mine - full
                out[0, 2 * j + q] = jnp.where(near, full, turn(raised)).astype(BF16)
                out[1, 2 * j + q] = jnp.where(near, turn(full), raised).astype(BF16)

    def unpack(both, half, n):
        @pl.loop(n * size // 2, (n + 1) * size // 2)
        def _(j):
            for q in (0, 1):
                v = both[2 * j + q]
                sq_ref[half * HALF + q * PAIRS + j] = v[:, :B]
                ra_ref[half * HALF + q * PAIRS + j] = v[:, B:]

    copies = []
    for n in range(CUTS):
        finish(n)
        if n == 0:
            pl.semaphore_wait(barrier, 1)
        at = pl.ds(n * size, size)
        copy = pltpu.make_async_remote_copy(
            src_ref=out.at[1 - layer, at], dst_ref=got.at[at], send_sem=s_sem.at[n], recv_sem=r_sem.at[n],
            device_id=other, device_id_type=MESH,
        )
        copy.start()
        copies.append(copy)
    for n in range(CUTS):
        unpack(out.at[layer], layer, n)
    for n, copy in enumerate(copies):
        copy.wait_recv()
        unpack(got, 1 - layer, n)
    for copy in copies:
        copy.wait_send()


def swap(acc, a):
    out = jax.ShapeDtypeStruct((2 * HALF, B, B), BF16)
    return pl.pallas_call(
        swap_kernel,
        out_shape=(out, out),
        in_specs=[pl.BlockSpec(memory_space=pltpu.VMEM)] * 2,
        out_specs=(pl.BlockSpec(memory_space=pltpu.VMEM),) * 2,
        scratch_shapes=[
            pltpu.VMEM((2, HALF, B, W), BF16),
            pltpu.VMEM((HALF, B, W), BF16),
            pltpu.SemaphoreType.DMA((CUTS,)),
            pltpu.SemaphoreType.DMA((CUTS,)),
        ],
        compiler_params=pltpu.CompilerParams(
            collective_id=1, has_side_effects=True, vmem_limit_bytes=24 << 20
        ),
        name="swap",
    )(acc, a)


def on_device(density, pattern):
    a, b = gather(density.reshape(2 * HALF, B, B), pattern.reshape(1, 2 * HALF))
    squared, raised = swap(multiply(a, b), a)
    return squared.reshape(density.shape), raised.reshape(density.shape)


def solution(mesh):
    placed = (P("row", "col", "layer", None, None), P("row", "col", "layer"))
    return jax.shard_map(
        on_device,
        mesh=mesh,
        in_specs=placed,
        out_specs=(P("row", "col", "layer", None, None), P("row", "col", "layer", None, None)),
        check_vma=False,
    )
```

```python
import jax
import jax.numpy as jnp
from jax import lax
from jax.experimental import pallas as pl
from jax.experimental.pallas import tpu as pltpu
from jax.sharding import PartitionSpec as P

MESH = pl.DeviceIdType.MESH
F32 = jnp.float32
BF16 = jnp.bfloat16

B = 64
W = 2 * B
HALF = 32
PAIRS = HALF // 2
BODY = PAIRS * B
UNIT = BODY + PAIRS
TILES = 16
CUT = (0, 528, 1040)
PIECES = range(len(CUT) - 1)
YS, ZS, XS = 4, 4, 4


def lanes(rows):
    return lax.broadcasted_iota(jnp.int32, (rows, W), 1)


def gather_kernel(d_ref, p_ref, a_ref, b_ref,
                  e_s, e_r, z_s, z_r, y_s, y_r, f_s, f_r, g_s, g_r, x_s, x_r, t_s, t_r, l_s):
    layer, row, col = lax.axis_index("layer"), lax.axis_index("row"), lax.axis_index("col")
    x, core = row // 2, row % 2
    y, z = col // ZS, col % ZS
    twin = x * 2 + 1 - core
    step, away = 1 + 2 * core, 3 - 2 * layer

    def at_z(d):
        return y * ZS + (z + d) % ZS

    def at_y(d):
        return ((y + d) % YS) * ZS + z

    def at_x(d):
        return ((x + d) % XS) * 2 + core

    other = {"layer": 1 - layer}
    aside = {"layer": 1 - layer, "col": at_z(away)}
    peers = [other, aside, {"row": twin}]
    peers += [{"col": at_z(d)} for d in (1, 3)]
    peers += [{"col": at_y(d)} for d in (1, 3)]
    peers += [{"row": at_x(d)} for d in (1, 2, 3)]
    barrier = pltpu.get_barrier_semaphore()
    for peer in peers:
        pl.semaphore_signal(barrier, inc=1, device_id=peer, device_id_type=MESH)

    number = p_ref[...].astype(F32)
    lane = lax.broadcasted_iota(jnp.int32, (PAIRS, B), 1)
    sub = lax.broadcasted_iota(jnp.int32, (PAIRS, B), 0)

    def entry(first):
        return jnp.sum(jnp.where(lane == sub + first, number, 0.0), axis=1, keepdims=True)

    for h in (0, 1):
        @pl.loop(0, PAIRS, unroll=4)
        def _(j):
            b_ref[2 * row + h, layer, pl.ds(pl.multiple_of(j * B, B), B), :] = jnp.concatenate(
                [d_ref[h * HALF + j], d_ref[h * HALF + PAIRS + j]], axis=1
            )

        b_ref[2 * row + h, layer, pl.ds(BODY, PAIRS), :] = jnp.where(
            lanes(PAIRS) < B, entry(h * HALF), entry(h * HALF + PAIRS)
        ).astype(BF16)

    pl.semaphore_wait(barrier, len(peers))

    sends, local = [], []

    def send(src, dst, ssem, rsem, peer):
        copy = pltpu.make_async_remote_copy(
            src_ref=src, dst_ref=dst, send_sem=ssem, recv_sem=rsem, device_id=peer, device_id_type=MESH
        )
        copy.start()
        sends.append(copy)

    def arrived(ref, ssem, rsem):
        pltpu.make_async_remote_copy(
            src_ref=ref, dst_ref=ref, send_sem=ssem, recv_sem=rsem, device_id=other, device_id_type=MESH
        ).wait_recv()

    offset = (0, 4 - step, step, 0, away, 4 - away, 2, 2)
    whose = (layer, layer, layer, 1 - layer, 1 - layer, 1 - layer, 1 - layer, layer)

    def a_at(dy, n):
        return a_ref.at[((y + dy) % YS) * ZS + (z + offset[n]) % ZS, whose[n]]

    def b_at(there, h, s):
        return b_ref.at[2 * there + h, s]

    mine, theirs = b_at(row, layer, layer), b_at(row, 1 - layer, layer)

    def sense(n):
        return 1 + 2 * ((n + core) % 2)

    def piece(ref, p):
        return ref.at[pl.ds(CUT[p], CUT[p + 1] - CUT[p])]

    def to_y(src, n, p):
        for k, d in enumerate((sense(n), 4 - sense(n))):
            send(piece(src, p), piece(a_at(0, n), p), y_s.at[n, k, p], y_r.at[n, k, p], {"col": at_y(d)})

    def to_x(src, h, own):
        n = h * 2 + own
        for d in (1, 3, 2):
            send(src, src, x_s.at[n, d - 1], x_r.at[n, d - 1], {"row": at_x(d)})

    def to_twin(src, n):
        send(src, src, t_s.at[n], t_r.at[n], {"row": twin})

    def keep(src, n):
        copy = pltpu.make_async_copy(src, a_at(0, n), l_s.at[n // 3])
        copy.start()
        local.append(copy)

    def to_z(src, dst, n, p, peer):
        send(piece(src, p), piece(dst, p), z_s.at[n, p], z_r.at[n, p], peer)

    def pass_far(ref, m, p):
        send(piece(ref, p), piece(ref, p), g_s.at[m, p], g_r.at[m, p], {"col": at_z(step)})

    for p in PIECES:
        to_z(theirs, theirs, 3, p, other)
        to_z(theirs, a_at(0, 0), 4, p, aside)
        to_z(mine, a_at(0, 0), 1, p, {"col": at_z(step)})
        to_y(mine, 0, p)
        to_z(mine, a_at(0, 0), 2, p, {"col": at_z(4 - step)})
    to_x(mine, 0, 0)
    to_x(theirs, 1, 0)
    to_twin(mine, 0)
    to_twin(theirs, 2)
    keep(mine, 0)

    def on_z(n, p):
        ref = b_at(row, layer, 1 - layer) if n == 3 else a_at(0, n)
        arrived(piece(ref, p), z_s.at[n, p], z_r.at[n, p])
        if n == 3:
            to_z(ref, a_at(0, 3), 5, p, {"col": at_z(away)})
        if n == 1:
            pass_far(ref, 0, p)
        if n == 4:
            to_z(ref, ref, 6, p, {"col": at_z(4 - away)})
        to_y(ref, n, p)

    def on_y(n, k, p):
        d = (4 - sense(n), sense(n))[k]
        ref = a_at(d, n)
        arrived(piece(ref, p), y_s.at[n, k, p], y_r.at[n, k, p])
        if n == 1:
            pass_far(ref, 1 + k, p)
        if k == 0:
            send(piece(ref, p), piece(ref, p), f_s.at[n, p], f_r.at[n, p], {"col": at_y(sense(n))})

    def on_f(n, p):
        ref = a_at(2, n)
        arrived(piece(ref, p), f_s.at[n, p], f_r.at[n, p])
        if n == 1:
            pass_far(ref, 3, p)

    def on_far(m, p):
        arrived(piece(a_at((0, 4 - sense(1), sense(1), 2)[m], 7), p), g_s.at[m, p], g_r.at[m, p])

    def on_x(d, h, own):
        there = ((x + XS - d) % XS) * 2 + core
        ref = b_at(there, (layer, 1 - layer)[h], (layer, 1 - layer)[own])
        n = h * 2 + own
        arrived(ref, x_s.at[n, d - 1], x_r.at[n, d - 1])
        to_twin(ref, 4 + n * 3 + d - 1)

    for p in PIECES:
        on_z(3, p)
        if p == PIECES[-1]:
            send(mine, mine, e_s, e_r, other)
        on_z(1, p)
        on_y(0, 0, p)
        on_z(4, p)
    ref = b_at(row, layer, 1 - layer)
    to_x(ref, 0, 1)
    to_twin(ref, 1)
    keep(ref, 3)
    for p in PIECES:
        on_y(3, 0, p)
        on_y(1, 0, p)
        on_y(1, 1, p)
        on_z(2, p)
    for d in (1, 3):
        on_x(d, 0, 0)
    for p in PIECES:
        on_y(4, 0, p)
        on_f(1, p)
        on_z(5, p)
        on_z(6, p)
    for d in (1, 3):
        on_x(d, 1, 0)
    ref = b_at(row, 1 - layer, 1 - layer)
    arrived(ref, e_s, e_r)
    to_x(ref, 1, 1)
    to_twin(ref, 3)
    for p in PIECES:
        on_y(2, 0, p)
    on_x(2, 0, 0)
    on_x(2, 1, 0)
    for p in PIECES:
        on_y(5, 0, p)
    for d in (1, 3, 2):
        on_x(d, 0, 1)
    for p in PIECES:
        on_y(6, 0, p)
    for d in (1, 3, 2):
        on_x(d, 1, 1)
    for p in PIECES:
        for n in (0, 3, 4, 2, 5, 6):
            on_y(n, 1, p)
            on_f(n, p)
        for m in range(4):
            on_far(m, p)
    for n in range(4):
        h, s = (layer, 1 - layer)[n // 2], (layer, 1 - layer)[n % 2]
        arrived(b_at(twin, h, s), t_s.at[n], t_r.at[n])
        for d in (1, 2, 3):
            there = ((x + XS - d) % XS) * 2 + 1 - core
            m = 4 + n * 3 + d - 1
            arrived(b_at(there, h, s), t_s.at[m], t_r.at[m])
    for copy in sends:
        copy.wait_send()
    for copy in local:
        copy.wait()


def gather(d, p):
    wide = jax.ShapeDtypeStruct((TILES, 2, UNIT, W), BF16)
    dma = pltpu.SemaphoreType.DMA
    return pl.pallas_call(
        gather_kernel,
        out_shape=(wide, wide),
        in_specs=[pl.BlockSpec(memory_space=pltpu.VMEM)] * 2,
        out_specs=(pl.BlockSpec(memory_space=pltpu.VMEM),) * 2,
        scratch_shapes=[
            dma, dma,
            dma((7, len(PIECES))), dma((7, len(PIECES))),
            dma((7, 2, len(PIECES))), dma((7, 2, len(PIECES))),
            dma((7, len(PIECES))), dma((7, len(PIECES))),
            dma((4, len(PIECES))), dma((4, len(PIECES))),
            dma((4, 3)), dma((4, 3)),
            dma((16,)), dma((16,)),
            dma((2,)),
        ],
        compiler_params=pltpu.CompilerParams(
            collective_id=0, has_side_effects=True, vmem_limit_bytes=30 << 20
        ),
        name="gather",
    )(d, p)


CHUNK = W
MOST = TILES * 2 * HALF


def turn(v):
    return jnp.concatenate([v[:, B:], v[:, :B]], axis=1)


def pattern(ref, t):
    one = ref[t, 0, pl.ds(BODY, PAIRS), :].astype(F32)
    two = ref[t, 1, pl.ds(BODY, PAIRS), :].astype(F32)
    near = lanes(PAIRS) < B
    return jnp.concatenate([jnp.where(near, one, turn(two)), jnp.where(near, turn(one), two)], axis=0)


def in_row(block):
    sub = lax.broadcasted_iota(jnp.int32, (HALF, W), 0)
    return jnp.sum(jnp.where(lanes(HALF) % B == sub, block, 0.0), axis=0, keepdims=True)


def match(a_ref, b_ref, codes, t, want):
    want_turned = turn(want)
    right = lanes(1) >= B
    used = lanes(1) % B < HALF
    inner = in_row(pattern(a_ref, t))
    table = pattern(b_ref, t)
    hot = inner == lax.broadcasted_iota(jnp.int32, (HALF, W), 0).astype(F32)
    own = jnp.sum(jnp.where(hot, table, 0.0), axis=0, keepdims=True)
    other = jnp.sum(jnp.where(hot, turn(table), 0.0), axis=0, keepdims=True)
    live = used & (inner >= 0)

    def same(u, v):
        return jnp.where(live & (u == v) & (v >= 0), 1, 0)

    f0, f1 = same(own, want), same(other, want)
    f2, f3 = same(own, want_turned), same(other, want_turned)
    flags = (
        jnp.where(right, f3, f0) + 2 * jnp.where(right, f0, f3)
        + 4 * jnp.where(right, f2, f1) + 8 * jnp.where(right, f1, f2)
    )
    place = lanes(1) % B + jnp.where(right, HALF, 0) + t * 2 * HALF
    codes[pl.ds(t, 1), :] = jnp.where(flags > 0, flags + 16 * inner.astype(jnp.int32) + 512 * place, 0)


GROUP = 8


def multiply_kernel(a_ref, b_ref, acc, codes, ranks, hits, listed, sem):
    col = lax.axis_index("col")
    want = in_row(pattern(a_ref, col))
    for t in range(TILES):
        match(a_ref, b_ref, codes, t, want)

    code = codes[...]
    hit = jnp.where(code > 0, 1.0, 0.0).astype(BF16)
    down = lax.broadcasted_iota(jnp.int32, (W, W), 0)
    before = jnp.where(down < lanes(W), 1.0, 0.0).astype(BF16)
    in_tile = jnp.dot(hit, before, preferred_element_type=F32)
    of_tile = jnp.dot(hit, jnp.ones((W, W), BF16), preferred_element_type=F32)
    tiles = lax.broadcasted_iota(jnp.int32, (TILES, TILES), 0)
    above = jnp.where(lax.broadcasted_iota(jnp.int32, (TILES, TILES), 1) < tiles, 1.0, 0.0).astype(BF16)
    rank = in_tile + jnp.dot(above, of_tile.astype(BF16), preferred_element_type=F32)
    ranks[...] = jnp.where(code > 0, rank, -1.0)
    total = jnp.sum(of_tile, axis=0, keepdims=True).astype(jnp.int32)
    hits[...] = jnp.broadcast_to(total, (8, W))

    def enlist(c):
        wanted = (down + c * CHUNK).astype(F32)
        found = jnp.zeros((CHUNK, W), F32)
        for t in range(TILES):
            found += jnp.where(ranks[pl.ds(t, 1), :] == wanted, codes[pl.ds(t, 1), :].astype(F32), 0.0)
        column = jnp.sum(found, axis=1, keepdims=True)
        line = jnp.sum(jnp.where(down == lanes(W), column, 0.0), axis=0, keepdims=True)
        hits[pl.ds(0, 1), :] = line.astype(jnp.int32)
        copy = pltpu.make_async_copy(hits, listed, sem)
        copy.start()
        return copy

    def product(code):
        k, place = (code // 16) % HALF, code // 512
        t, s, j = place // (2 * HALF), (place // HALF) % 2, place % HALF
        at = pl.ds(pl.multiple_of(k % PAIRS * B, B), B)
        from_row = pl.ds(pl.multiple_of(j % PAIRS * B, B), B)
        far, q = k // PAIRS, j // PAIRS
        near = lanes(1) < B

        def pick(bit_left, bit_right):
            return jnp.where(near, (code // bit_left) % 2, (code // bit_right) % 2).astype(F32)

        stay = b_ref[t, far, at, :].astype(F32)
        move = b_ref[t, 1 - far, at, :].astype(F32)
        here = lanes(B) // B == far
        straight = jnp.where(here, stay, turn(move))
        crossed = jnp.where(here, move, turn(stay))
        w = (straight * pick(1, 2) + crossed * pick(4, 8)).astype(BF16)
        a = a_ref[t, s, from_row, :] * jnp.where(lanes(1) // B == q, 1.0, 0.0).astype(BF16)
        return j, jnp.dot(a, jnp.concatenate([w, w], axis=0), preferred_element_type=F32)

    def run(number):
        @pl.loop(0, (number + GROUP - 1) // GROUP)
        def _(n):
            for j, value in [product(listed[0, n * GROUP + m]) for m in range(GROUP)]:
                acc[j] += value

    first = enlist(0)

    @pl.loop(0, HALF)
    def _(j):
        acc[j] = jnp.zeros((B, W), F32)

    first.wait()
    number = listed[1, 0]
    run(jnp.minimum(number, CHUNK))

    @pl.loop(1, MOST // CHUNK)
    def _(c):
        @pl.when(c * CHUNK < number)
        def _():
            enlist(c).wait()
            run(jnp.minimum(number - c * CHUNK, CHUNK))


def multiply(a, b):
    return pl.pallas_call(
        multiply_kernel,
        out_shape=jax.ShapeDtypeStruct((HALF, B, W), F32),
        in_specs=[pl.BlockSpec(memory_space=pltpu.VMEM)] * 2,
        out_specs=pl.BlockSpec(memory_space=pltpu.VMEM),
        scratch_shapes=[
            pltpu.VMEM((TILES, W), jnp.int32),
            pltpu.VMEM((TILES, W), F32),
            pltpu.VMEM((8, W), jnp.int32),
            pltpu.SMEM((8, W), jnp.int32),
            pltpu.SemaphoreType.DMA,
        ],
        compiler_params=pltpu.CompilerParams(vmem_limit_bytes=32 << 20),
        name="multiply",
    )(a, b)


CUTS = 8


def swap_kernel(acc, a_ref, sq_ref, ra_ref, out, got, s_sem, r_sem):
    layer, col = lax.axis_index("layer"), lax.axis_index("col")
    other = {"layer": 1 - layer}
    barrier = pltpu.get_barrier_semaphore()
    pl.semaphore_signal(barrier, inc=1, device_id=other, device_id_type=MESH)
    size = HALF // CUTS
    near = lanes(1) < B

    def finish(n):
        @pl.loop(n * size // 2, (n + 1) * size // 2)
        def _(j):
            at = pl.ds(pl.multiple_of(j * B, B), B)
            one, two = a_ref[col, 0, at, :].astype(F32), a_ref[col, 1, at, :].astype(F32)
            for q in (0, 1):
                full = acc[q * PAIRS + j]
                mine = jnp.where(near, one, turn(two)) if q == 0 else jnp.where(near, turn(one), two)
                raised = 2.0 * mine - full
                out[0, 2 * j + q] = jnp.where(near, full, turn(raised)).astype(BF16)
                out[1, 2 * j + q] = jnp.where(near, turn(full), raised).astype(BF16)

    def unpack(both, half, n):
        @pl.loop(n * size // 2, (n + 1) * size // 2)
        def _(j):
            for q in (0, 1):
                v = both[2 * j + q]
                sq_ref[half * HALF + q * PAIRS + j] = v[:, :B]
                ra_ref[half * HALF + q * PAIRS + j] = v[:, B:]

    copies = []
    for n in range(CUTS):
        finish(n)
        if n == 0:
            pl.semaphore_wait(barrier, 1)
        at = pl.ds(n * size, size)
        copy = pltpu.make_async_remote_copy(
            src_ref=out.at[1 - layer, at], dst_ref=got.at[at], send_sem=s_sem.at[n], recv_sem=r_sem.at[n],
            device_id=other, device_id_type=MESH,
        )
        copy.start()
        copies.append(copy)
    for n in range(CUTS):
        unpack(out.at[layer], layer, n)
    for n, copy in enumerate(copies):
        copy.wait_recv()
        unpack(got, 1 - layer, n)
    for copy in copies:
        copy.wait_send()


def swap(acc, a):
    out = jax.ShapeDtypeStruct((2 * HALF, B, B), BF16)
    return pl.pallas_call(
        swap_kernel,
        out_shape=(out, out),
        in_specs=[pl.BlockSpec(memory_space=pltpu.VMEM)] * 2,
        out_specs=(pl.BlockSpec(memory_space=pltpu.VMEM),) * 2,
        scratch_shapes=[
            pltpu.VMEM((2, HALF, B, W), BF16),
            pltpu.VMEM((HALF, B, W), BF16),
            pltpu.SemaphoreType.DMA((CUTS,)),
            pltpu.SemaphoreType.DMA((CUTS,)),
        ],
        compiler_params=pltpu.CompilerParams(
            collective_id=1, has_side_effects=True, vmem_limit_bytes=24 << 20
        ),
        name="swap",
    )(acc, a)


def on_device(density, pattern):
    a, b = gather(density.reshape(2 * HALF, B, B), pattern.reshape(1, 2 * HALF))
    squared, raised = swap(multiply(a, b), a)
    return squared.reshape(density.shape), raised.reshape(density.shape)


def solution(mesh):
    placed = (P("row", "col", "layer", None, None), P("row", "col", "layer"))
    return jax.shard_map(
        on_device,
        mesh=mesh,
        in_specs=placed,
        out_specs=(P("row", "col", "layer", None, None), P("row", "col", "layer", None, None)),
        check_vma=False,
    )
```

```python
import jax
import jax.numpy as jnp
from jax import lax
from jax.experimental import pallas as pl
from jax.experimental.pallas import tpu as pltpu
from jax.sharding import PartitionSpec as P

MESH = pl.DeviceIdType.MESH
F32 = jnp.float32
BF16 = jnp.bfloat16

B = 64
W = 2 * B
HALF = 32
PAIRS = HALF // 2
BODY = PAIRS * B
UNIT = BODY + PAIRS
TILES = 16
CUT = (0, 528, 1040)
PIECES = range(len(CUT) - 1)
YS, ZS, XS = 4, 4, 4


def lanes(rows):
    return lax.broadcasted_iota(jnp.int32, (rows, W), 1)


def gather_kernel(d_hbm, p_hbm, a_ref, b_ref, d_ref, p_ref,
                  e_s, e_r, z_s, z_r, y_s, y_r, f_s, f_r, g_s, g_r, x_s, x_r, t_s, t_r, l_s, i_s):
    loads = [pltpu.make_async_copy(p_hbm, p_ref, i_s.at[4])]
    for n in range(4):
        at = pl.ds(n * PAIRS, PAIRS)
        loads.append(pltpu.make_async_copy(d_hbm.at[at], d_ref.at[at], i_s.at[n]))
    for copy in loads:
        copy.start()
    layer, row, col = lax.axis_index("layer"), lax.axis_index("row"), lax.axis_index("col")
    x, core = row // 2, row % 2
    y, z = col // ZS, col % ZS
    twin = x * 2 + 1 - core
    step, away = 1 + 2 * core, 3 - 2 * layer

    def at_z(d):
        return y * ZS + (z + d) % ZS

    def at_y(d):
        return ((y + d) % YS) * ZS + z

    def at_x(d):
        return ((x + d) % XS) * 2 + core

    other = {"layer": 1 - layer}
    aside = {"layer": 1 - layer, "col": at_z(away)}
    peers = [other, aside, {"row": twin}]
    peers += [{"col": at_z(d)} for d in (1, 3)]
    peers += [{"col": at_y(d)} for d in (1, 3)]
    peers += [{"row": at_x(d)} for d in (1, 2, 3)]
    barrier = pltpu.get_barrier_semaphore()
    for peer in peers:
        pl.semaphore_signal(barrier, inc=1, device_id=peer, device_id_type=MESH)

    loads[0].wait()

    number = p_ref[...].astype(F32)
    lane = lax.broadcasted_iota(jnp.int32, (PAIRS, B), 1)
    sub = lax.broadcasted_iota(jnp.int32, (PAIRS, B), 0)

    def entry(first):
        return jnp.sum(jnp.where(lane == sub + first, number, 0.0), axis=1, keepdims=True)

    for h in (0, 1):
        for copy in loads[1 + 2 * h:3 + 2 * h]:
            copy.wait()

        @pl.loop(0, PAIRS, unroll=4)
        def _(j):
            b_ref[2 * row + h, layer, pl.ds(pl.multiple_of(j * B, B), B), :] = jnp.concatenate(
                [d_ref[h * HALF + j], d_ref[h * HALF + PAIRS + j]], axis=1
            )

        b_ref[2 * row + h, layer, pl.ds(BODY, PAIRS), :] = jnp.where(
            lanes(PAIRS) < B, entry(h * HALF), entry(h * HALF + PAIRS)
        ).astype(BF16)

    pl.semaphore_wait(barrier, len(peers))

    sends, local = [], []

    def send(src, dst, ssem, rsem, peer):
        copy = pltpu.make_async_remote_copy(
            src_ref=src, dst_ref=dst, send_sem=ssem, recv_sem=rsem, device_id=peer, device_id_type=MESH
        )
        copy.start()
        sends.append(copy)

    def arrived(ref, ssem, rsem):
        pltpu.make_async_remote_copy(
            src_ref=ref, dst_ref=ref, send_sem=ssem, recv_sem=rsem, device_id=other, device_id_type=MESH
        ).wait_recv()

    offset = (0, 4 - step, step, 0, away, 4 - away, 2, 2)
    whose = (layer, layer, layer, 1 - layer, 1 - layer, 1 - layer, 1 - layer, layer)

    def a_at(dy, n):
        return a_ref.at[((y + dy) % YS) * ZS + (z + offset[n]) % ZS, whose[n]]

    def b_at(there, h, s):
        return b_ref.at[2 * there + h, s]

    mine, theirs = b_at(row, layer, layer), b_at(row, 1 - layer, layer)

    def sense(n):
        return 1 + 2 * ((n + core) % 2)

    def piece(ref, p):
        return ref.at[pl.ds(CUT[p], CUT[p + 1] - CUT[p])]

    def to_y(src, n, p):
        for k, d in enumerate((sense(n), 4 - sense(n))):
            send(piece(src, p), piece(a_at(0, n), p), y_s.at[n, k, p], y_r.at[n, k, p], {"col": at_y(d)})

    def to_x(src, h, own):
        n = h * 2 + own
        for d in (1, 3, 2):
            send(src, src, x_s.at[n, d - 1], x_r.at[n, d - 1], {"row": at_x(d)})

    def to_twin(src, n):
        send(src, src, t_s.at[n], t_r.at[n], {"row": twin})

    def keep(src, n):
        copy = pltpu.make_async_copy(src, a_at(0, n), l_s.at[n // 3])
        copy.start()
        local.append(copy)

    def to_z(src, dst, n, p, peer):
        send(piece(src, p), piece(dst, p), z_s.at[n, p], z_r.at[n, p], peer)

    def pass_far(ref, m, p):
        send(piece(ref, p), piece(ref, p), g_s.at[m, p], g_r.at[m, p], {"col": at_z(step)})

    for p in PIECES:
        to_z(theirs, theirs, 3, p, other)
        to_z(theirs, a_at(0, 0), 4, p, aside)
        to_z(mine, a_at(0, 0), 1, p, {"col": at_z(step)})
        to_y(mine, 0, p)
        to_z(mine, a_at(0, 0), 2, p, {"col": at_z(4 - step)})
    to_x(mine, 0, 0)
    to_x(theirs, 1, 0)
    to_twin(mine, 0)
    to_twin(theirs, 2)
    keep(mine, 0)

    def on_z(n, p):
        ref = b_at(row, layer, 1 - layer) if n == 3 else a_at(0, n)
        arrived(piece(ref, p), z_s.at[n, p], z_r.at[n, p])
        if n == 3:
            to_z(ref, a_at(0, 3), 5, p, {"col": at_z(away)})
        if n == 1:
            pass_far(ref, 0, p)
        if n == 4:
            to_z(ref, ref, 6, p, {"col": at_z(4 - away)})
        to_y(ref, n, p)

    def on_y(n, k, p):
        d = (4 - sense(n), sense(n))[k]
        ref = a_at(d, n)
        arrived(piece(ref, p), y_s.at[n, k, p], y_r.at[n, k, p])
        if n == 1:
            pass_far(ref, 1 + k, p)
        if k == 0:
            send(piece(ref, p), piece(ref, p), f_s.at[n, p], f_r.at[n, p], {"col": at_y(sense(n))})

    def on_f(n, p):
        ref = a_at(2, n)
        arrived(piece(ref, p), f_s.at[n, p], f_r.at[n, p])
        if n == 1:
            pass_far(ref, 3, p)

    def on_far(m, p):
        arrived(piece(a_at((0, 4 - sense(1), sense(1), 2)[m], 7), p), g_s.at[m, p], g_r.at[m, p])

    def on_x(d, h, own):
        there = ((x + XS - d) % XS) * 2 + core
        ref = b_at(there, (layer, 1 - layer)[h], (layer, 1 - layer)[own])
        n = h * 2 + own
        arrived(ref, x_s.at[n, d - 1], x_r.at[n, d - 1])
        to_twin(ref, 4 + n * 3 + d - 1)

    for p in PIECES:
        on_z(3, p)
        if p == PIECES[-1]:
            send(mine, mine, e_s, e_r, other)
        on_z(1, p)
        on_y(0, 0, p)
        on_z(4, p)
    ref = b_at(row, layer, 1 - layer)
    to_x(ref, 0, 1)
    to_twin(ref, 1)
    keep(ref, 3)
    for p in PIECES:
        on_y(3, 0, p)
        on_y(1, 0, p)
        on_y(1, 1, p)
        on_z(2, p)
    for d in (1, 3):
        on_x(d, 0, 0)
    for p in PIECES:
        on_y(4, 0, p)
        on_f(1, p)
        on_z(5, p)
        on_z(6, p)
    for d in (1, 3):
        on_x(d, 1, 0)
    ref = b_at(row, 1 - layer, 1 - layer)
    arrived(ref, e_s, e_r)
    to_x(ref, 1, 1)
    to_twin(ref, 3)
    for p in PIECES:
        on_y(2, 0, p)
    on_x(2, 0, 0)
    on_x(2, 1, 0)
    for p in PIECES:
        on_y(5, 0, p)
    for d in (1, 3, 2):
        on_x(d, 0, 1)
    for p in PIECES:
        on_y(6, 0, p)
    for d in (1, 3, 2):
        on_x(d, 1, 1)
    for p in PIECES:
        for n in (0, 3, 4, 2, 5, 6):
            on_y(n, 1, p)
            on_f(n, p)
        for m in range(4):
            on_far(m, p)
    for n in range(4):
        h, s = (layer, 1 - layer)[n // 2], (layer, 1 - layer)[n % 2]
        arrived(b_at(twin, h, s), t_s.at[n], t_r.at[n])
        for d in (1, 2, 3):
            there = ((x + XS - d) % XS) * 2 + 1 - core
            m = 4 + n * 3 + d - 1
            arrived(b_at(there, h, s), t_s.at[m], t_r.at[m])
    for copy in sends:
        copy.wait_send()
    for copy in local:
        copy.wait()


def gather(d, p):
    wide = jax.ShapeDtypeStruct((TILES, 2, UNIT, W), BF16)
    dma = pltpu.SemaphoreType.DMA
    return pl.pallas_call(
        gather_kernel,
        out_shape=(wide, wide),
        in_specs=[pl.BlockSpec(memory_space=pltpu.HBM)] * 2,
        out_specs=(pl.BlockSpec(memory_space=pltpu.VMEM),) * 2,
        scratch_shapes=[
            pltpu.VMEM((2 * HALF, B, B), BF16),
            pltpu.VMEM((1, 2 * HALF), jnp.int32),
            dma, dma,
            dma((7, len(PIECES))), dma((7, len(PIECES))),
            dma((7, 2, len(PIECES))), dma((7, 2, len(PIECES))),
            dma((7, len(PIECES))), dma((7, len(PIECES))),
            dma((4, len(PIECES))), dma((4, len(PIECES))),
            dma((4, 3)), dma((4, 3)),
            dma((16,)), dma((16,)),
            dma((2,)),
            dma((5,)),
        ],
        compiler_params=pltpu.CompilerParams(
            collective_id=0, has_side_effects=True, vmem_limit_bytes=30 << 20
        ),
        name="gather",
    )(pltpu.with_memory_space_constraint(d, pltpu.HBM), pltpu.with_memory_space_constraint(p, pltpu.HBM))


CHUNK = W
MOST = TILES * 2 * HALF


def turn(v):
    return jnp.concatenate([v[:, B:], v[:, :B]], axis=1)


def pattern(ref, t):
    one = ref[t, 0, pl.ds(BODY, PAIRS), :].astype(F32)
    two = ref[t, 1, pl.ds(BODY, PAIRS), :].astype(F32)
    near = lanes(PAIRS) < B
    return jnp.concatenate([jnp.where(near, one, turn(two)), jnp.where(near, turn(one), two)], axis=0)


def in_row(block):
    sub = lax.broadcasted_iota(jnp.int32, (HALF, W), 0)
    return jnp.sum(jnp.where(lanes(HALF) % B == sub, block, 0.0), axis=0, keepdims=True)


def match(a_ref, b_ref, codes, t, want):
    want_turned = turn(want)
    right = lanes(1) >= B
    used = lanes(1) % B < HALF
    inner = in_row(pattern(a_ref, t))
    table = pattern(b_ref, t)
    hot = inner == lax.broadcasted_iota(jnp.int32, (HALF, W), 0).astype(F32)
    own = jnp.sum(jnp.where(hot, table, 0.0), axis=0, keepdims=True)
    other = jnp.sum(jnp.where(hot, turn(table), 0.0), axis=0, keepdims=True)
    live = used & (inner >= 0)

    def same(u, v):
        return jnp.where(live & (u == v) & (v >= 0), 1, 0)

    f0, f1 = same(own, want), same(other, want)
    f2, f3 = same(own, want_turned), same(other, want_turned)
    flags = (
        jnp.where(right, f3, f0) + 2 * jnp.where(right, f0, f3)
        + 4 * jnp.where(right, f2, f1) + 8 * jnp.where(right, f1, f2)
    )
    place = lanes(1) % B + jnp.where(right, HALF, 0) + t * 2 * HALF
    codes[pl.ds(t, 1), :] = jnp.where(flags > 0, flags + 16 * inner.astype(jnp.int32) + 512 * place, 0)


GROUP = 8


def multiply_kernel(a_ref, b_ref, acc, codes, ranks, hits, listed, sem):
    col = lax.axis_index("col")
    want = in_row(pattern(a_ref, col))
    for t in range(TILES):
        match(a_ref, b_ref, codes, t, want)

    code = codes[...]
    hit = jnp.where(code > 0, 1.0, 0.0).astype(BF16)
    down = lax.broadcasted_iota(jnp.int32, (W, W), 0)
    before = jnp.where(down < lanes(W), 1.0, 0.0).astype(BF16)
    in_tile = jnp.dot(hit, before, preferred_element_type=F32)
    of_tile = jnp.dot(hit, jnp.ones((W, W), BF16), preferred_element_type=F32)
    tiles = lax.broadcasted_iota(jnp.int32, (TILES, TILES), 0)
    above = jnp.where(lax.broadcasted_iota(jnp.int32, (TILES, TILES), 1) < tiles, 1.0, 0.0).astype(BF16)
    rank = in_tile + jnp.dot(above, of_tile.astype(BF16), preferred_element_type=F32)
    ranks[...] = jnp.where(code > 0, rank, -1.0)
    total = jnp.sum(of_tile, axis=0, keepdims=True).astype(jnp.int32)
    hits[...] = jnp.broadcast_to(total, (8, W))

    def enlist(c):
        wanted = (down + c * CHUNK).astype(F32)
        found = jnp.zeros((CHUNK, W), F32)
        for t in range(TILES):
            found += jnp.where(ranks[pl.ds(t, 1), :] == wanted, codes[pl.ds(t, 1), :].astype(F32), 0.0)
        column = jnp.sum(found, axis=1, keepdims=True)
        line = jnp.sum(jnp.where(down == lanes(W), column, 0.0), axis=0, keepdims=True)
        hits[pl.ds(0, 1), :] = line.astype(jnp.int32)
        copy = pltpu.make_async_copy(hits, listed, sem)
        copy.start()
        return copy

    def product(code):
        k, place = (code // 16) % HALF, code // 512
        t, s, j = place // (2 * HALF), (place // HALF) % 2, place % HALF
        at = pl.ds(pl.multiple_of(k % PAIRS * B, B), B)
        from_row = pl.ds(pl.multiple_of(j % PAIRS * B, B), B)
        far, q = k // PAIRS, j // PAIRS
        near = lanes(1) < B

        def pick(bit_left, bit_right):
            return jnp.where(near, (code // bit_left) % 2, (code // bit_right) % 2).astype(F32)

        stay = b_ref[t, far, at, :].astype(F32)
        move = b_ref[t, 1 - far, at, :].astype(F32)
        here = lanes(B) // B == far
        straight = jnp.where(here, stay, turn(move))
        crossed = jnp.where(here, move, turn(stay))
        w = (straight * pick(1, 2) + crossed * pick(4, 8)).astype(BF16)
        a = a_ref[t, s, from_row, :] * jnp.where(lanes(1) // B == q, 1.0, 0.0).astype(BF16)
        return j, jnp.dot(a, jnp.concatenate([w, w], axis=0), preferred_element_type=F32)

    def run(number):
        @pl.loop(0, (number + GROUP - 1) // GROUP)
        def _(n):
            for j, value in [product(listed[0, n * GROUP + m]) for m in range(GROUP)]:
                acc[j] += value

    first = enlist(0)

    @pl.loop(0, HALF)
    def _(j):
        acc[j] = jnp.zeros((B, W), F32)

    first.wait()
    number = listed[1, 0]
    run(jnp.minimum(number, CHUNK))

    @pl.loop(1, MOST // CHUNK)
    def _(c):
        @pl.when(c * CHUNK < number)
        def _():
            enlist(c).wait()
            run(jnp.minimum(number - c * CHUNK, CHUNK))


def multiply(a, b):
    return pl.pallas_call(
        multiply_kernel,
        out_shape=jax.ShapeDtypeStruct((HALF, B, W), F32),
        in_specs=[pl.BlockSpec(memory_space=pltpu.VMEM)] * 2,
        out_specs=pl.BlockSpec(memory_space=pltpu.VMEM),
        scratch_shapes=[
            pltpu.VMEM((TILES, W), jnp.int32),
            pltpu.VMEM((TILES, W), F32),
            pltpu.VMEM((8, W), jnp.int32),
            pltpu.SMEM((8, W), jnp.int32),
            pltpu.SemaphoreType.DMA,
        ],
        compiler_params=pltpu.CompilerParams(vmem_limit_bytes=32 << 20),
        name="multiply",
    )(a, b)


CUTS = 8


def swap_kernel(acc, a_ref, sq_ref, ra_ref, out, got, s_sem, r_sem):
    layer, col = lax.axis_index("layer"), lax.axis_index("col")
    other = {"layer": 1 - layer}
    barrier = pltpu.get_barrier_semaphore()
    pl.semaphore_signal(barrier, inc=1, device_id=other, device_id_type=MESH)
    size = HALF // CUTS
    near = lanes(1) < B

    def finish(n):
        @pl.loop(n * size // 2, (n + 1) * size // 2)
        def _(j):
            at = pl.ds(pl.multiple_of(j * B, B), B)
            one, two = a_ref[col, 0, at, :].astype(F32), a_ref[col, 1, at, :].astype(F32)
            for q in (0, 1):
                full = acc[q * PAIRS + j]
                mine = jnp.where(near, one, turn(two)) if q == 0 else jnp.where(near, turn(one), two)
                raised = 2.0 * mine - full
                out[0, 2 * j + q] = jnp.where(near, full, turn(raised)).astype(BF16)
                out[1, 2 * j + q] = jnp.where(near, turn(full), raised).astype(BF16)

    def unpack(both, half, n):
        @pl.loop(n * size // 2, (n + 1) * size // 2)
        def _(j):
            for q in (0, 1):
                v = both[2 * j + q]
                sq_ref[half * HALF + q * PAIRS + j] = v[:, :B]
                ra_ref[half * HALF + q * PAIRS + j] = v[:, B:]

    copies = []
    for n in range(CUTS):
        finish(n)
        if n == 0:
            pl.semaphore_wait(barrier, 1)
        at = pl.ds(n * size, size)
        copy = pltpu.make_async_remote_copy(
            src_ref=out.at[1 - layer, at], dst_ref=got.at[at], send_sem=s_sem.at[n], recv_sem=r_sem.at[n],
            device_id=other, device_id_type=MESH,
        )
        copy.start()
        copies.append(copy)
    for n in range(CUTS):
        unpack(out.at[layer], layer, n)
    for n, copy in enumerate(copies):
        copy.wait_recv()
        unpack(got, 1 - layer, n)
    for copy in copies:
        copy.wait_send()


def swap(acc, a):
    out = jax.ShapeDtypeStruct((2 * HALF, B, B), BF16)
    return pl.pallas_call(
        swap_kernel,
        out_shape=(out, out),
        in_specs=[pl.BlockSpec(memory_space=pltpu.VMEM)] * 2,
        out_specs=(pl.BlockSpec(memory_space=pltpu.VMEM),) * 2,
        scratch_shapes=[
            pltpu.VMEM((2, HALF, B, W), BF16),
            pltpu.VMEM((HALF, B, W), BF16),
            pltpu.SemaphoreType.DMA((CUTS,)),
            pltpu.SemaphoreType.DMA((CUTS,)),
        ],
        compiler_params=pltpu.CompilerParams(
            collective_id=1, has_side_effects=True, vmem_limit_bytes=24 << 20
        ),
        name="swap",
    )(acc, a)


def on_device(density, pattern):
    a, b = gather(density.reshape(2 * HALF, B, B), pattern.reshape(1, 2 * HALF))
    squared, raised = swap(multiply(a, b), a)
    return squared.reshape(density.shape), raised.reshape(density.shape)


def solution(mesh):
    placed = (P("row", "col", "layer", None, None), P("row", "col", "layer"))
    return jax.shard_map(
        on_device,
        mesh=mesh,
        in_specs=placed,
        out_specs=(P("row", "col", "layer", None, None), P("row", "col", "layer", None, None)),
        check_vma=False,
    )
```

```python
import jax
import jax.numpy as jnp
from jax import lax
from jax.experimental import pallas as pl
from jax.experimental.pallas import tpu as pltpu
from jax.sharding import PartitionSpec as P

MESH = pl.DeviceIdType.MESH
F32 = jnp.float32
BF16 = jnp.bfloat16

B = 64
W = 2 * B
HALF = 32
PAIRS = HALF // 2
BODY = PAIRS * B
UNIT = BODY + PAIRS
TILES = 16
CUT = (0, 528, 1040)
PIECES = range(len(CUT) - 1)
YS, ZS, XS = 4, 4, 4


def lanes(rows):
    return lax.broadcasted_iota(jnp.int32, (rows, W), 1)


def gather_kernel(d_hbm, p_hbm, a_ref, b_ref, d_ref, p_ref,
                  e_s, e_r, z_s, z_r, y_s, y_r, f_s, f_r, g_s, g_r, x_s, x_r, t_s, t_r, l_s, i_s):
    loads = [pltpu.make_async_copy(p_hbm, p_ref, i_s.at[4])]
    for n in range(4):
        at = pl.ds(n * PAIRS, PAIRS)
        loads.append(pltpu.make_async_copy(d_hbm.at[at], d_ref.at[at], i_s.at[n]))
    for copy in loads:
        copy.start()
    layer, row, col = lax.axis_index("layer"), lax.axis_index("row"), lax.axis_index("col")
    x, core = row // 2, row % 2
    y, z = col // ZS, col % ZS
    twin = x * 2 + 1 - core
    step, away = 1 + 2 * core, 3 - 2 * layer

    def at_z(d):
        return y * ZS + (z + d) % ZS

    def at_y(d):
        return ((y + d) % YS) * ZS + z

    def at_x(d):
        return ((x + d) % XS) * 2 + core

    other = {"layer": 1 - layer}
    aside = {"layer": 1 - layer, "col": at_z(away)}
    peers = [other, aside, {"row": twin}]
    peers += [{"col": at_z(d)} for d in (1, 3)]
    peers += [{"col": at_y(d)} for d in (1, 3)]
    peers += [{"row": at_x(d)} for d in (1, 2, 3)]
    barrier = pltpu.get_barrier_semaphore()
    for peer in peers:
        pl.semaphore_signal(barrier, inc=1, device_id=peer, device_id_type=MESH)

    loads[0].wait()

    number = p_ref[...].astype(F32)
    lane = lax.broadcasted_iota(jnp.int32, (PAIRS, B), 1)
    sub = lax.broadcasted_iota(jnp.int32, (PAIRS, B), 0)

    def entry(first):
        return jnp.sum(jnp.where(lane == sub + first, number, 0.0), axis=1, keepdims=True)

    for h in (0, 1):
        for copy in loads[1 + 2 * h:3 + 2 * h]:
            copy.wait()

        @pl.loop(0, PAIRS, unroll=4)
        def _(j):
            b_ref[2 * row + h, layer, pl.ds(pl.multiple_of(j * B, B), B), :] = jnp.concatenate(
                [d_ref[h * HALF + j], d_ref[h * HALF + PAIRS + j]], axis=1
            )

        b_ref[2 * row + h, layer, pl.ds(BODY, PAIRS), :] = jnp.where(
            lanes(PAIRS) < B, entry(h * HALF), entry(h * HALF + PAIRS)
        ).astype(BF16)

    pl.semaphore_wait(barrier, len(peers))

    sends, local = [], []

    def send(src, dst, ssem, rsem, peer):
        copy = pltpu.make_async_remote_copy(
            src_ref=src, dst_ref=dst, send_sem=ssem, recv_sem=rsem, device_id=peer, device_id_type=MESH
        )
        copy.start()
        sends.append(copy)

    def arrived(ref, ssem, rsem):
        pltpu.make_async_remote_copy(
            src_ref=ref, dst_ref=ref, send_sem=ssem, recv_sem=rsem, device_id=other, device_id_type=MESH
        ).wait_recv()

    offset = (0, 4 - step, step, 0, away, 4 - away, 2, 2)
    whose = (layer, layer, layer, 1 - layer, 1 - layer, 1 - layer, 1 - layer, layer)

    def a_at(dy, n):
        return a_ref.at[((y + dy) % YS) * ZS + (z + offset[n]) % ZS, whose[n]]

    def b_at(there, h, s):
        return b_ref.at[2 * there + h, s]

    mine, theirs = b_at(row, layer, layer), b_at(row, 1 - layer, layer)

    def sense(n):
        return 1 + 2 * ((n + core) % 2)

    def piece(ref, p):
        return ref.at[pl.ds(CUT[p], CUT[p + 1] - CUT[p])]

    def to_y(src, n, p):
        for k, d in enumerate((sense(n), 4 - sense(n))):
            send(piece(src, p), piece(a_at(0, n), p), y_s.at[n, k, p], y_r.at[n, k, p], {"col": at_y(d)})

    def to_x(src, h, own):
        n = h * 2 + own
        for d in (1, 3, 2):
            send(src, src, x_s.at[n, d - 1], x_r.at[n, d - 1], {"row": at_x(d)})

    def to_twin(src, n):
        send(src, src, t_s.at[n], t_r.at[n], {"row": twin})

    def keep(src, n):
        copy = pltpu.make_async_copy(src, a_at(0, n), l_s.at[n // 3])
        copy.start()
        local.append(copy)

    def to_z(src, dst, n, p, peer):
        send(piece(src, p), piece(dst, p), z_s.at[n, p], z_r.at[n, p], peer)

    def pass_far(ref, m, p):
        send(piece(ref, p), piece(ref, p), g_s.at[m, p], g_r.at[m, p], {"col": at_z(step)})

    for p in PIECES:
        to_z(theirs, theirs, 3, p, other)
        to_z(theirs, a_at(0, 0), 4, p, aside)
        to_z(mine, a_at(0, 0), 1, p, {"col": at_z(step)})
        to_y(mine, 0, p)
        to_z(mine, a_at(0, 0), 2, p, {"col": at_z(4 - step)})
    to_x(mine, 0, 0)
    to_x(theirs, 1, 0)
    to_twin(mine, 0)
    to_twin(theirs, 2)
    keep(mine, 0)

    def on_z(n, p):
        ref = b_at(row, layer, 1 - layer) if n == 3 else a_at(0, n)
        arrived(piece(ref, p), z_s.at[n, p], z_r.at[n, p])
        if n == 3:
            to_z(ref, a_at(0, 3), 5, p, {"col": at_z(away)})
        if n == 1:
            pass_far(ref, 0, p)
        if n == 4:
            to_z(ref, ref, 6, p, {"col": at_z(4 - away)})
        to_y(ref, n, p)

    def on_y(n, k, p):
        d = (4 - sense(n), sense(n))[k]
        ref = a_at(d, n)
        arrived(piece(ref, p), y_s.at[n, k, p], y_r.at[n, k, p])
        if n == 1:
            pass_far(ref, 1 + k, p)
        if k == 0:
            send(piece(ref, p), piece(ref, p), f_s.at[n, p], f_r.at[n, p], {"col": at_y(sense(n))})

    def on_f(n, p):
        ref = a_at(2, n)
        arrived(piece(ref, p), f_s.at[n, p], f_r.at[n, p])
        if n == 1:
            pass_far(ref, 3, p)

    def on_far(m, p):
        arrived(piece(a_at((0, 4 - sense(1), sense(1), 2)[m], 7), p), g_s.at[m, p], g_r.at[m, p])

    def on_x(d, h, own):
        there = ((x + XS - d) % XS) * 2 + core
        ref = b_at(there, (layer, 1 - layer)[h], (layer, 1 - layer)[own])
        n = h * 2 + own
        arrived(ref, x_s.at[n, d - 1], x_r.at[n, d - 1])
        to_twin(ref, 4 + n * 3 + d - 1)

    for p in PIECES:
        on_z(3, p)
        if p == PIECES[-1]:
            send(mine, mine, e_s, e_r, other)
        on_z(1, p)
        on_y(0, 0, p)
        on_z(4, p)
    ref = b_at(row, layer, 1 - layer)
    to_x(ref, 0, 1)
    to_twin(ref, 1)
    keep(ref, 3)
    for p in PIECES:
        on_y(3, 0, p)
        on_y(1, 0, p)
        on_y(1, 1, p)
        on_z(2, p)
    for d in (1, 3):
        on_x(d, 0, 0)
    for p in PIECES:
        on_y(4, 0, p)
        on_f(1, p)
        on_z(5, p)
        on_z(6, p)
    for d in (1, 3):
        on_x(d, 1, 0)
    ref = b_at(row, 1 - layer, 1 - layer)
    arrived(ref, e_s, e_r)
    to_x(ref, 1, 1)
    to_twin(ref, 3)
    for p in PIECES:
        on_y(2, 0, p)
    on_x(2, 0, 0)
    on_x(2, 1, 0)
    for p in PIECES:
        on_y(5, 0, p)
    for d in (1, 3, 2):
        on_x(d, 0, 1)
    for p in PIECES:
        on_y(6, 0, p)
    for d in (1, 3, 2):
        on_x(d, 1, 1)
    for p in PIECES:
        for n in (0, 3, 4, 2, 5, 6):
            on_y(n, 1, p)
            on_f(n, p)
        for m in range(4):
            on_far(m, p)
    for n in range(4):
        h, s = (layer, 1 - layer)[n // 2], (layer, 1 - layer)[n % 2]
        arrived(b_at(twin, h, s), t_s.at[n], t_r.at[n])
        for d in (1, 2, 3):
            there = ((x + XS - d) % XS) * 2 + 1 - core
            m = 4 + n * 3 + d - 1
            arrived(b_at(there, h, s), t_s.at[m], t_r.at[m])
    for copy in sends:
        copy.wait_send()
    for copy in local:
        copy.wait()


def gather(d, p):
    wide = jax.ShapeDtypeStruct((TILES, 2, UNIT, W), BF16)
    dma = pltpu.SemaphoreType.DMA
    return pl.pallas_call(
        gather_kernel,
        out_shape=(wide, wide),
        in_specs=[pl.BlockSpec(memory_space=pltpu.HBM)] * 2,
        out_specs=(pl.BlockSpec(memory_space=pltpu.VMEM),) * 2,
        scratch_shapes=[
            pltpu.VMEM((2 * HALF, B, B), BF16),
            pltpu.VMEM((1, 2 * HALF), jnp.int32),
            dma, dma,
            dma((7, len(PIECES))), dma((7, len(PIECES))),
            dma((7, 2, len(PIECES))), dma((7, 2, len(PIECES))),
            dma((7, len(PIECES))), dma((7, len(PIECES))),
            dma((4, len(PIECES))), dma((4, len(PIECES))),
            dma((4, 3)), dma((4, 3)),
            dma((16,)), dma((16,)),
            dma((2,)),
            dma((5,)),
        ],
        compiler_params=pltpu.CompilerParams(
            collective_id=0, has_side_effects=True, vmem_limit_bytes=30 << 20
        ),
        name="gather",
    )(pltpu.with_memory_space_constraint(d, pltpu.HBM), pltpu.with_memory_space_constraint(p, pltpu.HBM))


CHUNK = W
MOST = TILES * 2 * HALF


def turn(v):
    return jnp.concatenate([v[:, B:], v[:, :B]], axis=1)


def pattern(ref, t):
    one = ref[t, 0, pl.ds(BODY, PAIRS), :].astype(F32)
    two = ref[t, 1, pl.ds(BODY, PAIRS), :].astype(F32)
    near = lanes(PAIRS) < B
    return jnp.concatenate([jnp.where(near, one, turn(two)), jnp.where(near, turn(one), two)], axis=0)


def in_row(block):
    sub = lax.broadcasted_iota(jnp.int32, (HALF, W), 0)
    return jnp.sum(jnp.where(lanes(HALF) % B == sub, block, 0.0), axis=0, keepdims=True)


def match(a_ref, b_ref, codes, t, want):
    want_turned = turn(want)
    right = lanes(1) >= B
    used = lanes(1) % B < HALF
    inner = in_row(pattern(a_ref, t))
    table = pattern(b_ref, t)
    hot = inner == lax.broadcasted_iota(jnp.int32, (HALF, W), 0).astype(F32)
    own = jnp.sum(jnp.where(hot, table, 0.0), axis=0, keepdims=True)
    other = jnp.sum(jnp.where(hot, turn(table), 0.0), axis=0, keepdims=True)
    live = used & (inner >= 0)

    def same(u, v):
        return jnp.where(live & (u == v) & (v >= 0), 1, 0)

    f0, f1 = same(own, want), same(other, want)
    f2, f3 = same(own, want_turned), same(other, want_turned)
    flags = (
        jnp.where(right, f3, f0) + 2 * jnp.where(right, f0, f3)
        + 4 * jnp.where(right, f2, f1) + 8 * jnp.where(right, f1, f2)
    )
    place = lanes(1) % B + jnp.where(right, HALF, 0) + t * 2 * HALF
    codes[pl.ds(t, 1), :] = jnp.where(flags > 0, flags + 16 * inner.astype(jnp.int32) + 512 * place, 0)


GROUP = 8


def multiply_kernel(a_ref, b_ref, acc, codes, ranks, hits, listed, sem):
    col = lax.axis_index("col")
    want = in_row(pattern(a_ref, col))
    for t in range(TILES):
        match(a_ref, b_ref, codes, t, want)

    code = codes[...]
    hit = jnp.where(code > 0, 1.0, 0.0).astype(BF16)
    down = lax.broadcasted_iota(jnp.int32, (W, W), 0)
    before = jnp.where(down < lanes(W), 1.0, 0.0).astype(BF16)
    in_tile = jnp.dot(hit, before, preferred_element_type=F32)
    of_tile = jnp.dot(hit, jnp.ones((W, W), BF16), preferred_element_type=F32)
    tiles = lax.broadcasted_iota(jnp.int32, (TILES, TILES), 0)
    above = jnp.where(lax.broadcasted_iota(jnp.int32, (TILES, TILES), 1) < tiles, 1.0, 0.0).astype(BF16)
    rank = in_tile + jnp.dot(above, of_tile.astype(BF16), preferred_element_type=F32)
    ranks[...] = jnp.where(code > 0, rank, -1.0)
    total = jnp.sum(of_tile, axis=0, keepdims=True).astype(jnp.int32)
    hits[...] = jnp.broadcast_to(total, (8, W))

    def enlist(c):
        wanted = (down + c * CHUNK).astype(F32)
        found = jnp.zeros((CHUNK, W), F32)
        for t in range(TILES):
            found += jnp.where(ranks[pl.ds(t, 1), :] == wanted, codes[pl.ds(t, 1), :].astype(F32), 0.0)
        column = jnp.sum(found, axis=1, keepdims=True)
        line = jnp.sum(jnp.where(down == lanes(W), column, 0.0), axis=0, keepdims=True)
        hits[pl.ds(0, 1), :] = line.astype(jnp.int32)
        copy = pltpu.make_async_copy(hits, listed, sem)
        copy.start()
        return copy

    def product(code):
        k, place = (code // 16) % HALF, code // 512
        t, s, j = place // (2 * HALF), (place // HALF) % 2, place % HALF
        at = pl.ds(pl.multiple_of(k % PAIRS * B, B), B)
        from_row = pl.ds(pl.multiple_of(j % PAIRS * B, B), B)
        far, q = k // PAIRS, j // PAIRS
        near = lanes(1) < B

        def pick(bit_left, bit_right):
            return jnp.where(near, (code // bit_left) % 2, (code // bit_right) % 2).astype(F32)

        stay = b_ref[t, far, at, :].astype(F32)
        move = b_ref[t, 1 - far, at, :].astype(F32)
        here = lanes(B) // B == far
        straight = jnp.where(here, stay, turn(move))
        crossed = jnp.where(here, move, turn(stay))
        w = (straight * pick(1, 2) + crossed * pick(4, 8)).astype(BF16)
        a = a_ref[t, s, from_row, :] * jnp.where(lanes(1) // B == q, 1.0, 0.0).astype(BF16)
        return j, jnp.dot(a, jnp.concatenate([w, w], axis=0), preferred_element_type=F32)

    def run(number):
        @pl.loop(0, (number + GROUP - 1) // GROUP)
        def _(n):
            for j, value in [product(listed[0, n * GROUP + m]) for m in range(GROUP)]:
                acc[j] += value

    first = enlist(0)

    @pl.loop(0, HALF)
    def _(j):
        acc[j] = jnp.zeros((B, W), F32)

    first.wait()
    number = listed[1, 0]
    run(jnp.minimum(number, CHUNK))

    @pl.loop(1, MOST // CHUNK)
    def _(c):
        @pl.when(c * CHUNK < number)
        def _():
            enlist(c).wait()
            run(jnp.minimum(number - c * CHUNK, CHUNK))


def multiply(a, b):
    return pl.pallas_call(
        multiply_kernel,
        out_shape=jax.ShapeDtypeStruct((HALF, B, W), F32),
        in_specs=[pl.BlockSpec(memory_space=pltpu.VMEM)] * 2,
        out_specs=pl.BlockSpec(memory_space=pltpu.VMEM),
        scratch_shapes=[
            pltpu.VMEM((TILES, W), jnp.int32),
            pltpu.VMEM((TILES, W), F32),
            pltpu.VMEM((8, W), jnp.int32),
            pltpu.SMEM((8, W), jnp.int32),
            pltpu.SemaphoreType.DMA,
        ],
        compiler_params=pltpu.CompilerParams(vmem_limit_bytes=32 << 20),
        name="multiply",
    )(a, b)


CUTS = 8


def swap_kernel(acc, a_ref, sq_ref, ra_ref, out, got, s_sem, r_sem):
    layer, col = lax.axis_index("layer"), lax.axis_index("col")
    other = {"layer": 1 - layer}
    barrier = pltpu.get_barrier_semaphore()
    pl.semaphore_signal(barrier, inc=1, device_id=other, device_id_type=MESH)
    size = HALF // CUTS
    near = lanes(1) < B

    def finish(n):
        @pl.loop(n * size // 2, (n + 1) * size // 2)
        def _(j):
            at = pl.ds(pl.multiple_of(j * B, B), B)
            one, two = a_ref[col, 0, at, :].astype(F32), a_ref[col, 1, at, :].astype(F32)
            for q in (0, 1):
                full = acc[q * PAIRS + j]
                mine = jnp.where(near, one, turn(two)) if q == 0 else jnp.where(near, turn(one), two)
                raised = 2.0 * mine - full
                out[0, 2 * j + q] = jnp.where(near, full, turn(raised)).astype(BF16)
                out[1, 2 * j + q] = jnp.where(near, turn(full), raised).astype(BF16)

    def unpack(both, half, n):
        @pl.loop(n * size // 2, (n + 1) * size // 2)
        def _(j):
            for q in (0, 1):
                v = both[2 * j + q]
                sq_ref[half * HALF + q * PAIRS + j] = v[:, :B]
                ra_ref[half * HALF + q * PAIRS + j] = v[:, B:]

    copies = []
    for n in range(CUTS):
        finish(n)
        if n == 0:
            pl.semaphore_wait(barrier, 1)
        at = pl.ds(n * size, size)
        copy = pltpu.make_async_remote_copy(
            src_ref=out.at[1 - layer, at], dst_ref=got.at[at], send_sem=s_sem.at[n], recv_sem=r_sem.at[n],
            device_id=other, device_id_type=MESH,
        )
        copy.start()
        copies.append(copy)
    for n in range(CUTS):
        unpack(out.at[layer], layer, n)
    for n, copy in enumerate(copies):
        copy.wait_recv()
        unpack(got, 1 - layer, n)
    for copy in copies:
        copy.wait_send()


def swap(acc, a):
    out = jax.ShapeDtypeStruct((2 * HALF, B, B), BF16)
    return pl.pallas_call(
        swap_kernel,
        out_shape=(out, out),
        in_specs=[pl.BlockSpec(memory_space=pltpu.VMEM)] * 2,
        out_specs=(pl.BlockSpec(memory_space=pltpu.VMEM),) * 2,
        scratch_shapes=[
            pltpu.VMEM((2, HALF, B, W), BF16),
            pltpu.VMEM((HALF, B, W), BF16),
            pltpu.SemaphoreType.DMA((CUTS,)),
            pltpu.SemaphoreType.DMA((CUTS,)),
        ],
        compiler_params=pltpu.CompilerParams(
            collective_id=1, has_side_effects=True, vmem_limit_bytes=24 << 20
        ),
        name="swap",
    )(acc, a)


def store_kernel(sq_ref, ra_ref, sq_out, ra_out, sems):
    copies = []
    for n in range(4):
        at = pl.ds(n * PAIRS, PAIRS)
        copies.append(pltpu.make_async_copy(sq_ref.at[at], sq_out.at[at], sems.at[0, n]))
        copies.append(pltpu.make_async_copy(ra_ref.at[at], ra_out.at[at], sems.at[1, n]))
    for copy in copies:
        copy.start()
    for copy in copies:
        copy.wait()


def store(sq, ra):
    out = jax.ShapeDtypeStruct(sq.shape, BF16)
    return pl.pallas_call(
        store_kernel,
        out_shape=(out, out),
        in_specs=[pl.BlockSpec(memory_space=pltpu.VMEM)] * 2,
        out_specs=(pl.BlockSpec(memory_space=pl.ANY),) * 2,
        scratch_shapes=[pltpu.SemaphoreType.DMA((2, 4))],
        compiler_params=pltpu.CompilerParams(vmem_limit_bytes=4 << 20),
        name="store",
    )(sq, ra)


def on_device(density, pattern):
    a, b = gather(density.reshape(2 * HALF, B, B), pattern.reshape(1, 2 * HALF))
    squared, raised = store(*swap(multiply(a, b), a))
    return squared.reshape(density.shape), raised.reshape(density.shape)


def solution(mesh):
    placed = (P("row", "col", "layer", None, None), P("row", "col", "layer"))
    return jax.shard_map(
        on_device,
        mesh=mesh,
        in_specs=placed,
        out_specs=(P("row", "col", "layer", None, None), P("row", "col", "layer", None, None)),
        check_vma=False,
    )
```
